32 devices in a mesh: seq: 8 (over z, x), head: 4 (over y, core).
Axes of the slice: x: 2, y: 2, z: 4, core: 2. Of those that a mesh axis runs over, the one named last changes fastest.
Arguments:
- queries: bfloat16 [4096, 4096], P('seq', 'head'), may hold values from -0.3984375 to 0.3984375
- keys: bfloat16 [4096, 4096], P('seq', 'head'), may hold values from -0.3984375 to 0.3984375
- values: bfloat16 [4096, 1024], P('seq', 'head'), may hold values from -3 to 3
- out_grad: bfloat16 [4096, 1024], P('seq', 'head'), may hold values from -0.29882812 to 0.29882812
- transitions: bfloat16 [32, 256, 256], replicated, may hold values from -1 to 1, as said below
- gammas: float32 [16], P('head'), may hold values from 0.6 to 1
- regimes: int32 [16], replicated, may hold values from 0 to 31
- documents: int32 [16], replicated, may hold values from 0 to 2, never falling along the last dimension, each value on 1 to 8 neighbouring positions
Outputs:
- query_grad: bfloat16 [4096, 4096], P('seq', 'head')
- key_grad: bfloat16 [4096, 4096], P('seq', 'head')
- value_grad: bfloat16 [4096, 1024], P('seq', 'head')
- regime_grad: float32 [32, 256, 256], P('seq', 'head')
The draws below stay inside these ranges and needn't reach their ends.
Inputs may be any that keep to these rules, and one draw needn't show every extreme that they name: `transitions`: diagonal entries lie in 0.9 to 1.0, the others are small. `documents`: document numbers never fall; each document spans at most 8 blocks and one spans exactly that many.
All inputs are finite; a program needn't handle non-finite values.
Results may differ from the reference program's by a relative error of at most 0.005.
Values sent between devices are 32-bit elements; how exact they have to be, the bound alone decides.
No kernel may reach another device: no remote copies, remote signals or barrier semaphores. Data moves between devices by JAX's collectives and lax.ppermute only.
A program may use at most 64 MiB of HBM per device.

```python
import math
import jax
import jax.numpy as jnp
import numpy as np
from jax import lax

STATE = 256
HEADS = 16
HEAD_DIM = 64
REGIMES = 32
BLOCK = 256
TOKENS = 4096
BLOCKS = 16
DOCS = 3


def draw_transitions(key, part):
    diagonal_key, remainder_key = jax.random.split(key)
    diagonal = jax.random.uniform(diagonal_key, (REGIMES, STATE, 1), jnp.float32, 0.9, 1.0)
    spread = 0.2 / math.sqrt(STATE)
    remainder = jnp.clip(jax.random.normal(remainder_key, (REGIMES, STATE, STATE), jnp.float32) * spread, -4.0 * spread, 4.0 * spread)
    on_diagonal = lax.broadcasted_iota(jnp.int32, (STATE, STATE), 0) == lax.broadcasted_iota(jnp.int32, (STATE, STATE), 1)
    return jnp.where(on_diagonal[None], diagonal, remainder).astype(jnp.bfloat16)


def touch_ends(result, stream_key, low, largest):
    longest = result.shape.index(max(result.shape))
    spots = []
    for shift in (0, 1):
        where = [jax.random.randint(jax.random.fold_in(stream_key, axis), (), 0, length) for axis, length in enumerate(result.shape)]
        where[longest] = (where[longest] + shift) % result.shape[longest]
        spots.append(tuple(where))
    return result.at[spots[0]].set(low).at[spots[1]].set(largest)


def levels(key, extent, pieces, least, top_value):
    level = 1.0
    for axis_at, parts in pieces:
        heights = jax.random.uniform(jax.random.fold_in(jax.random.fold_in(key, 6), axis_at), (parts,), jnp.float32, least / len(pieces), top_value / len(pieces))
        level = level * jnp.repeat(jnp.exp(heights), extent[axis_at] // parts).reshape((-1,) + (1,) * (len(extent) - 1 - axis_at))
    return level


def split_up(number_of, total, most, lean):
    weights = [(1 << 20) // math.isqrt(grade ** lean) + 1 for grade in range(2, number_of + 1)]
    rest, counts = total - most - (number_of - 1), [1] * (number_of - 1)
    while rest > 0:
        movable = [i for i in range(number_of - 1) if counts[i] < most]
        whole, remaining = sum([weights[i] for i in movable]), rest
        for i in movable:
            addition = min(most - counts[i], max(1, remaining * weights[i] // whole), rest)
            counts[i] = counts[i] + addition
            rest = rest - addition
    return np.array([most] + counts)


def ragged(rng, count, total, limit, lean):
    if count == 2:
        one = jax.random.randint(rng, (), max(1, total - limit), min(limit, total - 1) + 1)
        return jnp.stack([one, total - one])
    tallies = jnp.asarray(split_up(count, total, limit, lean), jnp.int32)
    pairs = (count - 1) // 2
    donor, receiver = tallies[1:1 + 2 * pairs:2], tallies[2:2 + 2 * pairs:2]
    margin = jnp.minimum(donor - 1, limit - receiver)
    moved = jax.random.randint(jax.random.fold_in(rng, 1), (pairs,), 0, 1 << 20) % (margin + 1)
    tallies = tallies.at[1:1 + 2 * pairs:2].set(donor - moved).at[2:2 + 2 * pairs:2].set(receiver + moved)
    return tallies[jax.random.permutation(jax.random.fold_in(rng, 2), count)]


def bell_draw(own_key, extent, deviation, reach, pieces=(), kind=jnp.bfloat16):
    values = jax.random.normal(own_key, extent, jnp.float32) * deviation
    if len(pieces) > 0:
        values = levels(own_key, extent, pieces, -0.22, 0.18) * values
    return jnp.clip(values, min=-reach, max=reach).astype(kind)


def setup_inputs(seed: int = 0) -> dict:
    splits = jax.random.split(jax.random.key(seed), 9)
    queries = bell_draw(splits[0], (TOKENS, HEADS * STATE), 0.0625, 0.3984375, ((0, 8), (1, 4)))
    keys = bell_draw(splits[1], (TOKENS, HEADS * STATE), 0.0625, 0.3984375, ((0, 8), (1, 4)))
    values = bell_draw(splits[2], (TOKENS, HEADS * HEAD_DIM), 0.5, 3.0, ((0, 8), (1, 4)))
    out_grad = bell_draw(splits[3], (TOKENS, HEADS * HEAD_DIM), 0.05, 0.29882812, ((0, 8), (1, 4)))
    transitions = draw_transitions(jax.random.fold_in(splits[8], 71), 0)
    gammas = jnp.clip(jnp.exp(math.log(1.0) - 0.5108256 * jax.random.uniform(splits[5], (HEADS,), jnp.float32) ** levels(splits[5], (HEADS,), ((0, 4),), -0.2, 0.2)), 0.6, 1.0)
    regimes = touch_ends(jax.random.randint(splits[6], (BLOCKS,), 0, REGIMES), jax.random.fold_in(splits[6], 1), 0, REGIMES - 1).astype(jnp.int32)
    documents = jnp.searchsorted(jnp.cumsum(ragged(splits[7], DOCS, BLOCKS, BLOCKS // 2, 1)), jnp.arange(BLOCKS), side="right").astype(jnp.int32)
    return dict(queries=queries, keys=keys, values=values, out_grad=out_grad, transitions=transitions, gammas=gammas, regimes=regimes, documents=documents)


PRECISE = lax.Precision.HIGHEST


def rounded(array):
    return lax.optimization_barrier(array.astype(jnp.bfloat16)).astype(jnp.float32)


def reference(queries, keys, values, out_grad, transitions, gammas, regimes, documents):
    query_rows = queries.reshape(BLOCKS, BLOCK, HEADS, STATE).astype(jnp.float32)
    key_rows = keys.reshape(BLOCKS, BLOCK, HEADS, STATE).astype(jnp.float32)
    value_rows = values.reshape(BLOCKS, BLOCK, HEADS, HEAD_DIM).astype(jnp.float32)
    grad_rows = out_grad.reshape(BLOCKS, BLOCK, HEADS, HEAD_DIM).astype(jnp.float32)
    same_doc = (documents[1:] == documents[:-1]).astype(jnp.float32)
    kept = jnp.concatenate([jnp.zeros((1,), jnp.float32), same_doc])
    matrices = jnp.take(transitions, regimes, axis=0).astype(jnp.float32)
    decays = gammas.astype(jnp.float32)
    zero_state = jnp.zeros((HEADS, STATE, HEAD_DIM), jnp.float32)

    def forward(previous, inputs):
        matrix, keep_one, key_block, value_block = inputs
        factor = keep_one * decays
        entry = factor[:, None, None] * jnp.einsum("nm,hmp->hnp", matrix, previous, precision=PRECISE)
        update = jnp.einsum("lhn,lhp->hnp", key_block, value_block, precision=PRECISE)
        return entry + update, (entry, previous)

    _, (entries, befores) = lax.scan(forward, zero_state, (matrices, kept, key_rows, value_rows))

    def backward(carried, inputs):
        matrix, keep_one, query_block, grad_block = inputs
        total = jnp.einsum("lhn,lhp->hnp", query_block, grad_block, precision=PRECISE) + carried
        factor = keep_one * decays
        passed = factor[:, None, None] * jnp.einsum("nm,hnp->hmp", matrix, total, precision=PRECISE)
        return passed, (total, carried)

    _, (totals, leaving) = lax.scan(backward, zero_state, (matrices, kept, query_rows, grad_rows), reverse=True)

    terms = kept[:, None, None] * jnp.einsum("h,chnp,chmp->cnm", decays, totals, befores, precision=PRECISE)
    regime_grad = jax.ops.segment_sum(terms, regimes, num_segments=REGIMES)

    causal = jnp.arange(BLOCK)[:, None] >= jnp.arange(BLOCK)[None, :]

    def within(inputs):
        query_block, key_block, value_block, grad_block, entry, leave = inputs
        scores = jnp.einsum("lhn,shn->hls", query_block, key_block, precision=PRECISE)
        probs = rounded(jnp.where(causal[None], scores, 0.0))
        dots = jnp.einsum("lhp,shp->hls", grad_block, value_block, precision=PRECISE)
        dscore = rounded(jnp.where(causal[None], dots, 0.0))
        entry_b = rounded(entry)
        leave_b = rounded(leave)
        query_grad = jnp.einsum("lhp,hnp->lhn", grad_block, entry_b, precision=PRECISE) + jnp.einsum("hls,shn->lhn", dscore, key_block, precision=PRECISE)
        key_grad = jnp.einsum("shp,hnp->shn", value_block, leave_b, precision=PRECISE) + jnp.einsum("hls,lhn->shn", dscore, query_block, precision=PRECISE)
        value_grad = jnp.einsum("shn,hnp->shp", key_block, leave_b, precision=PRECISE) + jnp.einsum("hls,lhp->shp", probs, grad_block, precision=PRECISE)
        return (query_grad.astype(jnp.bfloat16), key_grad.astype(jnp.bfloat16), value_grad.astype(jnp.bfloat16))

    query_grad, key_grad, value_grad = lax.map(within, (query_rows, key_rows, value_rows, grad_rows, entries, leaving))
    return (query_grad.reshape(TOKENS, HEADS * STATE), key_grad.reshape(TOKENS, HEADS * STATE), value_grad.reshape(TOKENS, HEADS * HEAD_DIM), regime_grad)
```

```python
import functools

import jax
import jax.numpy as jnp
from jax import lax
from jax.experimental import pallas as pl
from jax.experimental.pallas import tpu as pltpu
from jax.sharding import PartitionSpec as P

STATE = 256
HEAD_DIM = 64
REGIMES = 32
BLOCK = 256

F32 = jnp.float32
BF16 = jnp.bfloat16
NN = (((1,), (0,)), ((), ()))
NT = (((1,), (1,)), ((), ()))
TN = (((0,), (0,)), ((), ()))
VMEM = pl.BlockSpec(memory_space=pltpu.VMEM)
SMEM = pl.BlockSpec(memory_space=pltpu.SMEM)
PARAMS = pltpu.CompilerParams(vmem_limit_bytes=48 << 20)


def dot(a, b, dims):
    return lax.dot_general(a, b, dims, preferred_element_type=F32)


def halves(x):
    high = x.astype(BF16)
    return high, (x - high.astype(F32)).astype(BF16)


def dot_exact(x, matrix, dims):
    high, low = halves(x)
    return dot(high, matrix, dims) + dot(low, matrix, dims)


def dot_pair(a, b, dims):
    return dot(a[0], b[0], dims) + (dot(a[0], b[1], dims) + dot(a[1], b[0], dims))


def kept_at(documents, block):
    before = documents[jnp.maximum(block - 1, 0)]
    same = jnp.where(documents[block] == before, 1.0, 0.0)
    return jnp.where(block > 0, same, 0.0).astype(F32)


def decay_column(gammas, first, count, power):
    parts = []
    for i in range(count):
        g = gammas[first + i]
        value = g
        for _ in range(power - 1):
            value = value * g
        parts.append(jnp.full((HEAD_DIM, 1), value, F32))
    return jnp.concatenate(parts, axis=0)


def local_kernel(blocks, heads, regimes, documents, pos, gammas, q, k, v, dy, *rest):
    mats, (update, source, sent, held) = rest[:blocks], rest[blocks:]
    seq = pos[0]
    rows = heads * HEAD_DIM
    half = rows // 2
    decay = decay_column(gammas, 0, heads, 1)
    for c in range(blocks):
        token = slice(c * BLOCK, (c + 1) * BLOCK)
        for h in range(heads):
            wide = slice(h * STATE, (h + 1) * STATE)
            narrow = slice(h * HEAD_DIM, (h + 1) * HEAD_DIM)
            update[c, narrow, :] = dot(v[token, narrow], k[token, wide], TN)
            source[c, narrow, :] = dot(dy[token, narrow], q[token, wide], TN)
    state = update[0]
    for c in range(1, blocks):
        factor = kept_at(documents, seq * blocks + c) * decay
        state = update[c] + factor * dot_exact(state, mats[c][0], NT)
    carried = None
    for c in reversed(range(blocks)):
        total = source[c] if carried is None else source[c] + carried
        factor = kept_at(documents, seq * blocks + c) * decay
        carried = factor * dot_exact(total, mats[c][0], NN)
    upper = lax.rem(seq, 2) == 1
    for i, value in enumerate((state, carried)):
        first, second = value[:half], value[half:]
        held[i] = jnp.where(upper, second, first)
        sent[i] = jnp.where(upper, first, second)


def maps_kernel(blocks, reach, last_block, regimes, documents, pos, transitions, device_maps, *far):
    seq = pos[0]
    level = lax.div(seq, 2)

    def device_map(device):
        result = None
        for c in range(blocks):
            block = jnp.clip(device * blocks + c, 0, last_block)
            mat = transitions[regimes[block]]
            kept = kept_at(documents, block)
            if result is None:
                result = mat.astype(F32)
            elif c == 1:
                result = dot(mat, result.astype(BF16), NN)
            else:
                high, low = halves(result)
                result = dot(mat, high, NN) + dot(mat, low, NN)
            result = result * kept
        return result

    def pair_map(at):
        low = halves(device_map(at * 2))
        high = halves(device_map(at * 2 + 1))
        return dot_pair(high, low, NN)

    for i in range(2):
        device_maps[i, 0], device_maps[i, 1] = halves(device_map(level * 2 + i))
    if reach > 1:
        far = far[0]
        forward = backward = None
        for distance in range(2, reach + 1):
            behind = pair_map(level - distance + 1)
            ahead = pair_map(level + distance - 1)
            if forward is None:
                forward, backward = behind, ahead
            else:
                forward = dot_pair(halves(forward), halves(behind), NN)
                backward = dot_pair(halves(ahead), halves(backward), NN)
            far[distance - 2, 0, 0], far[distance - 2, 0, 1] = halves(forward)
            far[distance - 2, 1, 0], far[distance - 2, 1, 1] = halves(backward)


def pair_kernel(blocks, heads, routes, pos, gammas, held, arrived, device_maps, *outs):
    seq = pos[0]
    level, upper = lax.div(seq, 2), lax.rem(seq, 2)
    is_upper = upper == 1
    decay = decay_column(gammas, upper * (heads // 2), heads // 2, blocks)
    ends = [jnp.where(is_upper, arrived[0], held[0]), jnp.where(is_upper, held[0], arrived[0])]
    starts = [jnp.where(is_upper, arrived[1], held[1]), jnp.where(is_upper, held[1], arrived[1])]
    low_map = (device_maps[0, 0], device_maps[0, 1])
    high_map = (device_maps[1, 0], device_maps[1, 1])
    forward = ends[1] + decay * dot_pair(halves(ends[0]), high_map, NT)
    backward = starts[0] + decay * dot_pair(halves(starts[1]), low_map, NN)
    for out, (distance, parity) in zip(outs, routes):
        ahead = lax.rem(lax.div(level, distance), 2) == parity
        out[...] = jnp.where(ahead, forward, backward)


def entry_kernel(blocks, heads, reach, routes, pos, gammas, held, arrived, device_maps, *rest):
    count = len(routes)
    received, (own, sent) = rest[:count], rest[-2:]
    far = rest[count] if reach > 1 else None
    seq = pos[0]
    level, upper = lax.div(seq, 2), lax.rem(seq, 2)
    is_upper = upper == 1
    decay = decay_column(gammas, upper * (heads // 2), heads // 2, blocks)
    found = dict(zip(routes, received))
    forward = backward = None
    for distance in range(1, reach + 1):
        even = found[distance, 0][...]
        odd = found[distance, 1][...] if (distance, 1) in found else jnp.zeros_like(even)
        flip = lax.rem(lax.div(level, distance), 2) == 1
        behind = jnp.where(flip, even, odd)
        ahead = jnp.where(flip, odd, even)
        if distance == 1:
            forward, backward = behind, ahead
        else:
            power = decay_column(
                gammas, upper * (heads // 2), heads // 2, 2 * blocks * (distance - 1)
            )
            i = distance - 2
            forward += power * dot_pair(halves(behind), (far[i, 0, 0], far[i, 0, 1]), NT)
            backward += power * dot_pair(halves(ahead), (far[i, 1, 0], far[i, 1, 1]), NN)
    low_map = (device_maps[0, 0], device_maps[0, 1])
    high_map = (device_maps[1, 0], device_maps[1, 1])
    low_end = jnp.where(is_upper, arrived[0], held[0])
    high_start = jnp.where(is_upper, held[1], arrived[1])
    inner_forward = low_end + decay * dot_pair(halves(forward), low_map, NT)
    inner_backward = high_start + decay * dot_pair(halves(backward), high_map, NN)
    own[0] = jnp.where(is_upper, inner_forward, forward)
    own[1] = jnp.where(is_upper, backward, inner_backward)
    sent[0] = jnp.where(is_upper, forward, inner_forward)
    sent[1] = jnp.where(is_upper, inner_backward, backward)


def terms_kernel(
    blocks, heads, ways, regimes, documents, pos, gammas, own, arrived, update, source, *rest
):
    mats, (entries, leaves, held, sent, term) = rest[:blocks], rest[blocks:]
    seq, head = pos[0], pos[1]
    upper = lax.rem(seq, 2) == 1
    decay = decay_column(gammas, 0, heads, 1)

    def whole(i):
        first = jnp.where(upper, arrived[i], own[i])
        second = jnp.where(upper, own[i], arrived[i])
        return jnp.concatenate([first, second], axis=0)

    before, carried = whole(0), whole(1)
    kept = [kept_at(documents, seq * blocks + c) for c in range(blocks)]
    befores, totals = [], []
    for c in range(blocks):
        befores.append(halves(before))
        high, low = befores[-1]
        entry = (kept[c] * decay) * (dot(high, mats[c][0], NT) + dot(low, mats[c][0], NT))
        entries[c] = entry.astype(BF16)
        before = entry + update[c]
    for c in reversed(range(blocks)):
        leaves[c] = carried.astype(BF16)
        total = source[c] + carried
        totals.insert(0, total)
        carried = (kept[c] * decay) * dot_exact(total, mats[c][0], NN)
    part = STATE // ways
    core = lax.rem(head, 2)
    for c in range(blocks):
        term[...] = dot_pair(halves((kept[c] * decay) * totals[c]), befores[c], TN)
        for i in range(ways // 2):
            held[c, i] = term[pl.ds(pl.multiple_of((2 * i + core) * part, part), part), :]
            sent[c, i] = term[pl.ds(pl.multiple_of((2 * i + 1 - core) * part, part), part), :]


def regime_kernel(blocks, owned, count, regimes, base, sources, *rest):
    pieces, out = rest[:count], rest[count]
    for r in range(owned):
        total = None
        for i in range(count):
            for c in range(blocks):
                block = jnp.maximum(sources[i], 0) * blocks + c
                match = (sources[i] >= 0) & (regimes[block] == base[0] + r)
                value = jnp.where(match, pieces[i][c], 0.0)
                total = value if total is None else total + value
        out[r] = total


def within_kernel(q, k, v, dy, entry, leave, dq, dk, dv):
    heads = v.shape[1] // HEAD_DIM
    causal = lax.broadcasted_iota(jnp.int32, (BLOCK, BLOCK), 0) >= lax.broadcasted_iota(
        jnp.int32, (BLOCK, BLOCK), 1
    )
    for h in range(heads):
        wide = slice(h * STATE, (h + 1) * STATE)
        narrow = slice(h * HEAD_DIM, (h + 1) * HEAD_DIM)
        qh, kh, vh, gh = q[:, wide], k[:, wide], v[:, narrow], dy[:, narrow]
        eh, lh = entry[0, narrow, :], leave[0, narrow, :]
        probs = jnp.where(causal, dot(qh, kh, NT), 0.0).astype(BF16)
        dscore = jnp.where(causal, dot(gh, vh, NT), 0.0).astype(BF16)
        dq[:, wide] = (dot(gh, eh, NN) + dot(dscore, kh, NN)).astype(BF16)
        dk[:, wide] = (dot(vh, lh, NN) + dot(dscore, qh, TN)).astype(BF16)
        dv[:, narrow] = (dot(kh, lh, NT) + dot(probs, gh, TN)).astype(BF16)


def swap(x, axis, by):
    count = lax.axis_size(axis)
    return lax.ppermute(x, axis, [(i, i ^ by) for i in range(count)])


def level_route(x, distance, parity):
    levels = lax.axis_size("seq") // 2
    pairs = []
    for low in range(levels - distance):
        if (low // distance) % 2 == parity:
            for side in range(2):
                a, b = 2 * low + side, 2 * (low + distance) + side
                pairs += [(a, b), (b, a)]
    return lax.ppermute(x, "seq", pairs)


def routes_up_to(reach, levels):
    return [
        (distance, parity)
        for distance in range(1, reach + 1)
        for parity in range(2)
        if any((low // distance) % 2 == parity for low in range(levels - distance))
    ]


def local(queries, keys, values, out_grad, transitions, gammas, regimes, documents):
    tokens_dev = queries.shape[0]
    heads = gammas.shape[0]
    blocks = tokens_dev // BLOCK
    all_blocks = documents.shape[0]
    devices, ways = lax.axis_size("seq"), lax.axis_size("head")
    levels = devices // 2
    rows = heads * HEAD_DIM
    half = rows // 2
    reach = min(levels - 1, -(-(all_blocks // 2 - 1) // (2 * blocks)))
    routes = routes_up_to(reach, levels)
    seq, head = lax.axis_index("seq"), lax.axis_index("head")
    pos = jnp.stack([seq, head]).astype(jnp.int32)

    def shape(*dims, dtype=F32):
        return jax.ShapeDtypeStruct(dims, dtype)

    def whole(x):
        return pl.BlockSpec(x.shape, lambda i, *_: (0,) * len(x.shape))

    def own_mats():
        return [
            pl.BlockSpec(
                (1, STATE, STATE),
                lambda i, regimes, documents, pos, c=c: (regimes[pos[0] * blocks + c], 0, 0),
            )
            for c in range(blocks)
        ]

    state_shape = shape(blocks, rows, STATE)
    half_shape = shape(2, half, STATE)
    outs = (state_shape, state_shape, half_shape, half_shape)
    update, source, sent, held = pl.pallas_call(
        functools.partial(local_kernel, blocks, heads),
        grid_spec=pltpu.PrefetchScalarGridSpec(
            num_scalar_prefetch=3,
            grid=(1,),
            in_specs=[SMEM] + [whole(x) for x in (queries, keys, values, out_grad)] + own_mats(),
            out_specs=[whole(x) for x in outs],
        ),
        out_shape=outs,
        compiler_params=PARAMS,
    )(regimes, documents, pos, gammas, queries, keys, values, out_grad, *[transitions] * blocks)

    arrived = swap(sent, "seq", 1)
    map_shapes = (shape(2, 2, STATE, STATE, dtype=BF16),)
    if reach > 1:
        map_shapes += (shape(reach - 1, 2, 2, STATE, STATE, dtype=BF16),)
    maps = pl.pallas_call(
        functools.partial(maps_kernel, blocks, reach, all_blocks - 1),
        in_specs=[SMEM, SMEM, SMEM, VMEM],
        out_specs=(VMEM,) * len(map_shapes),
        out_shape=map_shapes,
        compiler_params=PARAMS,
    )(regimes, documents, pos, transitions)

    trades = pl.pallas_call(
        functools.partial(pair_kernel, blocks, heads, routes),
        in_specs=[SMEM, SMEM, VMEM, VMEM, VMEM],
        out_specs=(VMEM,) * len(routes),
        out_shape=(shape(half, STATE),) * len(routes),
        compiler_params=PARAMS,
    )(pos, gammas, held, arrived, maps[0])
    received = [level_route(x, *route) for x, route in zip(trades, routes)]

    own, sent_entry = pl.pallas_call(
        functools.partial(entry_kernel, blocks, heads, reach, routes),
        in_specs=[SMEM, SMEM] + [VMEM] * (3 + len(received) + len(maps) - 1),
        out_specs=(VMEM, VMEM),
        out_shape=(half_shape, half_shape),
        compiler_params=PARAMS,
    )(pos, gammas, held, arrived, maps[0], *received, *maps[1:])
    arrived_entry = swap(sent_entry, "seq", 1)

    part = STATE // ways
    part_shape = shape(blocks, ways // 2, part, STATE)
    bf16_states = shape(blocks, rows, STATE, dtype=BF16)
    outs = (bf16_states, bf16_states, part_shape, part_shape)
    entries, leaves, held_term, sent_term = pl.pallas_call(
        functools.partial(terms_kernel, blocks, heads, ways),
        grid_spec=pltpu.PrefetchScalarGridSpec(
            num_scalar_prefetch=3,
            grid=(1,),
            in_specs=[SMEM]
            + [whole(x) for x in (own, arrived_entry, update, source)]
            + own_mats(),
            out_specs=[whole(x) for x in outs],
            scratch_shapes=[pltpu.VMEM((STATE, STATE), F32)],
        ),
        out_shape=outs,
        compiler_params=PARAMS,
    )(regimes, documents, pos, gammas, own, arrived_entry, update, source, *[transitions] * blocks)

    summed = held_term + swap(sent_term, "head", 1)
    by = 2
    while by < ways:
        split = summed.reshape(blocks, -1, 2, part, STATE)
        bit = lax.rem(lax.div(head, by), 2)
        going = lax.dynamic_index_in_dim(split, 1 - bit, 2, keepdims=False)
        staying = lax.dynamic_index_in_dim(split, bit, 2, keepdims=False)
        summed = staying + swap(going, "head", by)
        by *= 2
    summed = summed.reshape(blocks, part, STATE)

    level, side = lax.div(seq, 2), lax.rem(seq, 2)
    pieces, sources = [summed], [seq]
    for distance, parity in routes_up_to(levels - 1, levels):
        pieces.append(level_route(summed, distance, parity))
        lower = lax.rem(lax.div(level, distance), 2) == parity
        other = jnp.where(lower, level + distance, level - distance)
        valid = (other >= 0) & (other < levels)
        sources.append(jnp.where(valid, other * 2 + side, -1))
    sources = jnp.stack(sources).astype(jnp.int32)
    owned = REGIMES // devices

    def regime_sum(device):
        return pl.pallas_call(
            functools.partial(regime_kernel, blocks, owned, len(pieces)),
            in_specs=[SMEM] * 3 + [VMEM] * len(pieces),
            out_specs=VMEM,
            out_shape=shape(owned, part, STATE),
            compiler_params=PARAMS,
        )(regimes, jnp.reshape(device * owned, (1,)).astype(jnp.int32), sources, *pieces)

    regime_grad = regime_sum(seq) + swap(regime_sum(seq ^ 1), "seq", 1)

    wide = pl.BlockSpec((BLOCK, 2 * STATE), lambda c, h: (c, h))
    narrow = pl.BlockSpec((BLOCK, 2 * HEAD_DIM), lambda c, h: (c, h))
    states = pl.BlockSpec((1, 2 * HEAD_DIM, STATE), lambda c, h: (c, h, 0))
    query_grad, key_grad, value_grad = pl.pallas_call(
        within_kernel,
        grid=(blocks, heads // 2),
        in_specs=[wide, wide, narrow, narrow, states, states],
        out_specs=[wide, wide, narrow],
        out_shape=(
            shape(*queries.shape, dtype=BF16),
            shape(*keys.shape, dtype=BF16),
            shape(*values.shape, dtype=BF16),
        ),
        compiler_params=PARAMS,
        cost_estimate=pl.CostEstimate(
            flops=blocks * heads * 10 * BLOCK * BLOCK * STATE,
            bytes_accessed=6 << 20,
            transcendentals=0,
        ),
    )(queries, keys, values, out_grad, entries, leaves)
    return query_grad, key_grad, value_grad, regime_grad


def solution(mesh):
    in_specs = (
        P("seq", "head"),
        P("seq", "head"),
        P("seq", "head"),
        P("seq", "head"),
        P(),
        P("head"),
        P(),
        P(),
    )
    out_specs = (P("seq", "head"), P("seq", "head"), P("seq", "head"), P("seq", "head", None))
    return jax.shard_map(local, mesh=mesh, in_specs=in_specs, out_specs=out_specs, check_vma=False)
```

```python
import functools

import jax
import jax.numpy as jnp
from jax import lax
from jax.experimental import pallas as pl
from jax.experimental.pallas import tpu as pltpu
from jax.sharding import PartitionSpec as P

STATE = 256
HEAD_DIM = 64
REGIMES = 32
BLOCK = 256

F32 = jnp.float32
BF16 = jnp.bfloat16
NN = (((1,), (0,)), ((), ()))
NT = (((1,), (1,)), ((), ()))
TN = (((0,), (0,)), ((), ()))
VMEM = pl.BlockSpec(memory_space=pltpu.VMEM)
SMEM = pl.BlockSpec(memory_space=pltpu.SMEM)
HBM = pl.BlockSpec(memory_space=pltpu.HBM)
PARAMS = pltpu.CompilerParams(vmem_limit_bytes=48 << 20)


def dot(a, b, dims):
    return lax.dot_general(a, b, dims, preferred_element_type=F32)


def halves(x):
    high = x.astype(BF16)
    return high, (x - high.astype(F32)).astype(BF16)


def dot_exact(x, matrix, dims):
    high, low = halves(x)
    return dot(high, matrix, dims) + dot(low, matrix, dims)


def dot_pair(a, b, dims):
    return dot(a[0], b[0], dims) + (dot(a[0], b[1], dims) + dot(a[1], b[0], dims))


def kept_at(documents, block):
    before = documents[jnp.maximum(block - 1, 0)]
    same = jnp.where(documents[block] == before, 1.0, 0.0)
    return jnp.where(block > 0, same, 0.0).astype(F32)


def decay_column(gammas, first, count, power):
    parts = []
    for i in range(count):
        g = gammas[first + i]
        value = g
        for _ in range(power - 1):
            value = value * g
        parts.append(jnp.full((HEAD_DIM, 1), value, F32))
    return jnp.concatenate(parts, axis=0)


def local_kernel(
    blocks, heads, regimes_hbm, documents_hbm, gammas_hbm, transitions, q_hbm, k_hbm, v_hbm, dy_hbm,
    update, source, sent, held,
    regimes, documents, gammas, mats, q, k, v, dy, small_sems, mat_sems, row_sems, wide_sems,
):
    seq = lax.axis_index("seq")
    half = heads * HEAD_DIM // 2
    split = heads * STATE // 2
    small = [
        pltpu.make_async_copy(a, b, small_sems.at[i])
        for i, (a, b) in enumerate(
            ((regimes_hbm, regimes), (documents_hbm, documents), (gammas_hbm, gammas))
        )
    ]
    for copy in small:
        copy.start()
    rows, wide = {}, {}
    for i, (a, b, wide_a, wide_b) in enumerate(((v_hbm, v, k_hbm, k), (dy_hbm, dy, q_hbm, q))):
        for c in range(blocks):
            token = pl.ds(c * BLOCK, BLOCK)
            rows[i, c] = pltpu.make_async_copy(a.at[token], b.at[token], row_sems.at[i, c])
            rows[i, c].start()
            for j in range(2):
                at = (token, pl.ds(j * split, split))
                wide[i, c, j] = pltpu.make_async_copy(
                    wide_a.at[at], wide_b.at[at], wide_sems.at[i, c, j]
                )
                wide[i, c, j].start()
    small[0].wait()
    mat_copies = []
    for c in range(blocks):
        copy = pltpu.make_async_copy(
            transitions.at[regimes[seq * blocks + c]], mats.at[c], mat_sems.at[c]
        )
        copy.start()
        mat_copies.append(copy)
    for i, (out, narrow_in, wide_in) in enumerate(((update, v, k), (source, dy, q))):
        for c in range(blocks):
            token = slice(c * BLOCK, (c + 1) * BLOCK)
            rows[i, c].wait()
            for h in range(heads):
                if h % (heads // 2) == 0:
                    wide[i, c, h // (heads // 2)].wait()
                columns = slice(h * STATE, (h + 1) * STATE)
                narrow = slice(h * HEAD_DIM, (h + 1) * HEAD_DIM)
                out[c, narrow, :] = dot(narrow_in[token, narrow], wide_in[token, columns], TN)
    for copy in small[1:] + mat_copies:
        copy.wait()
    decay = decay_column(gammas, 0, heads, 1)
    state = update[0]
    for c in range(1, blocks):
        factor = kept_at(documents, seq * blocks + c) * decay
        state = update[c] + factor * dot_exact(state, mats[c], NT)
    carried = None
    for c in reversed(range(blocks)):
        total = source[c] if carried is None else source[c] + carried
        factor = kept_at(documents, seq * blocks + c) * decay
        carried = factor * dot_exact(total, mats[c], NN)
    upper = lax.rem(seq, 2) == 1
    for i, value in enumerate((state, carried)):
        first, second = value[:half], value[half:]
        held[i] = jnp.where(upper, second, first)
        sent[i] = jnp.where(upper, first, second)


def maps_kernel(blocks, reach, last_block, regimes, documents, pos, transitions, device_maps, *far):
    seq = pos[0]
    level = lax.div(seq, 2)

    def device_map(device):
        result = None
        for c in range(blocks):
            block = jnp.clip(device * blocks + c, 0, last_block)
            mat = transitions[regimes[block]]
            kept = kept_at(documents, block)
            if result is None:
                result = mat.astype(F32)
            elif c == 1:
                result = dot(mat, result.astype(BF16), NN)
            else:
                high, low = halves(result)
                result = dot(mat, high, NN) + dot(mat, low, NN)
            result = result * kept
        return result

    def pair_map(at):
        low = halves(device_map(at * 2))
        high = halves(device_map(at * 2 + 1))
        return dot_pair(high, low, NN)

    for i in range(2):
        device_maps[i, 0], device_maps[i, 1] = halves(device_map(level * 2 + i))
    if reach > 1:
        far = far[0]
        forward = backward = None
        for distance in range(2, reach + 1):
            behind = pair_map(level - distance + 1)
            ahead = pair_map(level + distance - 1)
            if forward is None:
                forward, backward = behind, ahead
            else:
                forward = dot_pair(halves(forward), halves(behind), NN)
                backward = dot_pair(halves(ahead), halves(backward), NN)
            far[distance - 2, 0, 0], far[distance - 2, 0, 1] = halves(forward)
            far[distance - 2, 1, 0], far[distance - 2, 1, 1] = halves(backward)


def pair_kernel(blocks, heads, routes, pos, gammas, held, arrived, device_maps, *outs):
    seq = pos[0]
    level, upper = lax.div(seq, 2), lax.rem(seq, 2)
    is_upper = upper == 1
    decay = decay_column(gammas, upper * (heads // 2), heads // 2, blocks)
    ends = [jnp.where(is_upper, arrived[0], held[0]), jnp.where(is_upper, held[0], arrived[0])]
    starts = [jnp.where(is_upper, arrived[1], held[1]), jnp.where(is_upper, held[1], arrived[1])]
    low_map = (device_maps[0, 0], device_maps[0, 1])
    high_map = (device_maps[1, 0], device_maps[1, 1])
    forward = ends[1] + decay * dot_pair(halves(ends[0]), high_map, NT)
    backward = starts[0] + decay * dot_pair(halves(starts[1]), low_map, NN)
    for out, (distance, parity) in zip(outs, routes):
        ahead = lax.rem(lax.div(level, distance), 2) == parity
        out[...] = jnp.where(ahead, forward, backward)


def entry_kernel(blocks, heads, reach, routes, pos, gammas, held, arrived, device_maps, *rest):
    count = len(routes)
    received, (own, sent) = rest[:count], rest[-2:]
    far = rest[count] if reach > 1 else None
    seq = pos[0]
    level, upper = lax.div(seq, 2), lax.rem(seq, 2)
    is_upper = upper == 1
    decay = decay_column(gammas, upper * (heads // 2), heads // 2, blocks)
    found = dict(zip(routes, received))
    forward = backward = None
    for distance in range(1, reach + 1):
        even = found[distance, 0][...]
        odd = found[distance, 1][...] if (distance, 1) in found else jnp.zeros_like(even)
        flip = lax.rem(lax.div(level, distance), 2) == 1
        behind = jnp.where(flip, even, odd)
        ahead = jnp.where(flip, odd, even)
        if distance == 1:
            forward, backward = behind, ahead
        else:
            power = decay_column(
                gammas, upper * (heads // 2), heads // 2, 2 * blocks * (distance - 1)
            )
            i = distance - 2
            forward += power * dot_pair(halves(behind), (far[i, 0, 0], far[i, 0, 1]), NT)
            backward += power * dot_pair(halves(ahead), (far[i, 1, 0], far[i, 1, 1]), NN)
    low_map = (device_maps[0, 0], device_maps[0, 1])
    high_map = (device_maps[1, 0], device_maps[1, 1])
    low_end = jnp.where(is_upper, arrived[0], held[0])
    high_start = jnp.where(is_upper, held[1], arrived[1])
    inner_forward = low_end + decay * dot_pair(halves(forward), low_map, NT)
    inner_backward = high_start + decay * dot_pair(halves(backward), high_map, NN)
    own[0] = jnp.where(is_upper, inner_forward, forward)
    own[1] = jnp.where(is_upper, backward, inner_backward)
    sent[0] = jnp.where(is_upper, forward, inner_forward)
    sent[1] = jnp.where(is_upper, inner_backward, backward)


def states_of(blocks, upper, kept, decay, own, arrived, update, source, mats):
    def whole(i):
        first = jnp.where(upper, arrived[i], own[i])
        second = jnp.where(upper, own[i], arrived[i])
        return jnp.concatenate([first, second], axis=0)

    before, carried = whole(0), whole(1)
    befores, entries, leaves, totals = [], [], [None] * blocks, [None] * blocks
    for c in range(blocks):
        befores.append(halves(before))
        high, low = befores[-1]
        entry = (kept[c] * decay) * (dot(high, mats[c][0], NT) + dot(low, mats[c][0], NT))
        entries.append(entry)
        before = entry + update[c]
    for c in reversed(range(blocks)):
        leaves[c] = carried
        totals[c] = source[c] + carried
        if c > 0:
            carried = (kept[c] * decay) * dot_exact(totals[c], mats[c][0], NN)
    return befores, entries, leaves, totals


def terms_kernel(
    blocks, heads, ways, regimes, documents, pos, gammas, own, arrived, update, source, *rest
):
    mats, (held, sent, term) = rest[:blocks], rest[blocks:]
    seq, head = pos[0], pos[1]
    decay = decay_column(gammas, 0, heads, 1)
    kept = [kept_at(documents, seq * blocks + c) for c in range(blocks)]
    befores, _, _, totals = states_of(
        blocks, lax.rem(seq, 2) == 1, kept, decay, own, arrived, update, source, mats
    )
    part = STATE // ways
    core = lax.rem(head, 2)
    for c in range(blocks):
        term[...] = dot_pair(halves((kept[c] * decay) * totals[c]), befores[c], TN)
        for i in range(ways // 2):
            held[c, i] = term[pl.ds(pl.multiple_of((2 * i + core) * part, part), part), :]
            sent[c, i] = term[pl.ds(pl.multiple_of((2 * i + 1 - core) * part, part), part), :]


def rounded_kernel(
    blocks, heads, regimes, documents, pos, gammas, own, arrived, update, source, *rest
):
    mats, (entries, leaves) = rest[:blocks], rest[blocks:]
    seq = pos[0]
    decay = decay_column(gammas, 0, heads, 1)
    kept = [kept_at(documents, seq * blocks + c) for c in range(blocks)]
    _, entry, leave, _ = states_of(
        blocks, lax.rem(seq, 2) == 1, kept, decay, own, arrived, update, source, mats
    )
    for c in range(blocks):
        entries[c] = entry[c].astype(BF16)
        leaves[c] = leave[c].astype(BF16)


def regime_kernel(blocks, owned, count, regimes, base, sources, *rest):
    pieces, out = rest[:count], rest[count]
    for r in range(owned):
        total = None
        for i in range(count):
            for c in range(blocks):
                match = regimes[sources[i] * blocks + c] == base[0] + r
                value = jnp.where(match, pieces[i][c], 0.0)
                total = value if total is None else total + value
        out[r] = total


def add_kernel(a, b, out):
    out[...] = a[...] + b[...]


def within_kernel(q, k, v, dy, entry, leave, dq, dk, dv):
    heads = v.shape[1] // HEAD_DIM
    causal = lax.broadcasted_iota(jnp.int32, (BLOCK, BLOCK), 0) >= lax.broadcasted_iota(
        jnp.int32, (BLOCK, BLOCK), 1
    )
    for h in range(heads):
        wide = slice(h * STATE, (h + 1) * STATE)
        narrow = slice(h * HEAD_DIM, (h + 1) * HEAD_DIM)
        qh, kh, vh, gh = q[:, wide], k[:, wide], v[:, narrow], dy[:, narrow]
        eh, lh = entry[0, narrow, :], leave[0, narrow, :]
        probs = jnp.where(causal, dot(qh, kh, NT), 0.0).astype(BF16)
        dscore = jnp.where(causal, dot(gh, vh, NT), 0.0).astype(BF16)
        dq[:, wide] = (dot(gh, eh, NN) + dot(dscore, kh, NN)).astype(BF16)
        dk[:, wide] = (dot(vh, lh, NN) + dot(dscore, qh, TN)).astype(BF16)
        dv[:, narrow] = (dot(kh, lh, NT) + dot(probs, gh, TN)).astype(BF16)


def swap(x, axis, by):
    count = lax.axis_size(axis)
    return lax.ppermute(x, axis, [(i, i ^ by) for i in range(count)])


def level_route(x, distance, parity):
    levels = lax.axis_size("seq") // 2
    pairs = []
    for low in range(levels - distance):
        if (low // distance) % 2 == parity:
            for side in range(2):
                a, b = 2 * low + side, 2 * (low + distance) + side
                pairs += [(a, b), (b, a)]
    return lax.ppermute(x, "seq", pairs)


def routes_up_to(reach, levels):
    return [
        (distance, parity)
        for distance in range(1, reach + 1)
        for parity in range(2)
        if any((low // distance) % 2 == parity for low in range(levels - distance))
    ]


def local(queries, keys, values, out_grad, transitions, gammas, regimes, documents):
    tokens_dev = queries.shape[0]
    heads = gammas.shape[0]
    blocks = tokens_dev // BLOCK
    all_blocks = documents.shape[0]
    devices, ways = lax.axis_size("seq"), lax.axis_size("head")
    levels = devices // 2
    rows = heads * HEAD_DIM
    half = rows // 2
    reach = min(levels - 1, -(-(all_blocks // 2 - 1) // (2 * blocks)))
    routes = routes_up_to(reach, levels)[::-1]
    seq, head = lax.axis_index("seq"), lax.axis_index("head")
    pos = jnp.stack([seq, head]).astype(jnp.int32)

    def shape(*dims, dtype=F32):
        return jax.ShapeDtypeStruct(dims, dtype)

    def whole(x):
        return pl.BlockSpec(x.shape, lambda i, *_: (0,) * len(x.shape))

    def own_mats():
        return [
            pl.BlockSpec(
                (1, STATE, STATE),
                lambda i, regimes, documents, pos, c=c: (regimes[pos[0] * blocks + c], 0, 0),
            )
            for c in range(blocks)
        ]

    state_shape = shape(blocks, rows, STATE)
    half_shape = shape(2, half, STATE)
    outs = (state_shape, state_shape, half_shape, half_shape)
    update, source, sent, held = pl.pallas_call(
        functools.partial(local_kernel, blocks, heads),
        in_specs=[HBM] * 8,
        out_specs=(VMEM,) * 4,
        out_shape=outs,
        scratch_shapes=[
            pltpu.SMEM(regimes.shape, jnp.int32),
            pltpu.SMEM(documents.shape, jnp.int32),
            pltpu.SMEM(gammas.shape, F32),
            pltpu.VMEM((blocks, STATE, STATE), BF16),
            pltpu.VMEM(queries.shape, BF16),
            pltpu.VMEM(keys.shape, BF16),
            pltpu.VMEM(values.shape, BF16),
            pltpu.VMEM(out_grad.shape, BF16),
            pltpu.SemaphoreType.DMA((3,)),
            pltpu.SemaphoreType.DMA((blocks,)),
            pltpu.SemaphoreType.DMA((2, blocks)),
            pltpu.SemaphoreType.DMA((2, blocks, 2)),
        ],
        compiler_params=pltpu.CompilerParams(vmem_limit_bytes=60 << 20),
    )(regimes, documents, gammas, transitions, queries, keys, values, out_grad)

    arrived = swap(sent, "seq", 1)
    map_shapes = (shape(2, 2, STATE, STATE, dtype=BF16),)
    if reach > 1:
        map_shapes += (shape(reach - 1, 2, 2, STATE, STATE, dtype=BF16),)
    maps = pl.pallas_call(
        functools.partial(maps_kernel, blocks, reach, all_blocks - 1),
        in_specs=[SMEM, SMEM, SMEM, VMEM],
        out_specs=(VMEM,) * len(map_shapes),
        out_shape=map_shapes,
        compiler_params=PARAMS,
    )(regimes, documents, pos, transitions)

    trades = pl.pallas_call(
        functools.partial(pair_kernel, blocks, heads, routes),
        in_specs=[SMEM, SMEM, VMEM, VMEM, VMEM],
        out_specs=(VMEM,) * len(routes),
        out_shape=(shape(half, STATE),) * len(routes),
        compiler_params=PARAMS,
    )(pos, gammas, held, arrived, maps[0])
    received = [level_route(x, *route) for x, route in zip(trades, routes)]

    own, sent_entry = pl.pallas_call(
        functools.partial(entry_kernel, blocks, heads, reach, routes),
        in_specs=[SMEM, SMEM] + [VMEM] * (3 + len(received) + len(maps) - 1),
        out_specs=(VMEM, VMEM),
        out_shape=(half_shape, half_shape),
        compiler_params=PARAMS,
    )(pos, gammas, held, arrived, maps[0], *received, *maps[1:])
    arrived_entry = swap(sent_entry, "seq", 1)

    part = STATE // ways
    part_shape = shape(blocks, ways // 2, part, STATE)
    bf16_states = shape(blocks, rows, STATE, dtype=BF16)
    states = (own, arrived_entry, update, source)

    def states_call(kernel, states, outs, scratch):
        return pl.pallas_call(
            kernel,
            grid_spec=pltpu.PrefetchScalarGridSpec(
                num_scalar_prefetch=3,
                grid=(1,),
                in_specs=[SMEM] + [whole(x) for x in states] + own_mats(),
                out_specs=[whole(x) for x in outs],
                scratch_shapes=scratch,
            ),
            out_shape=outs,
            compiler_params=PARAMS,
        )(regimes, documents, pos, gammas, *states, *[transitions] * blocks)

    held_term, sent_term = states_call(
        functools.partial(terms_kernel, blocks, heads, ways),
        states,
        (part_shape, part_shape),
        [pltpu.VMEM((STATE, STATE), F32)],
    )

    summed = held_term + swap(sent_term, "head", 1)
    by = 2
    while by < ways:
        split = summed.reshape(blocks, -1, 2, part, STATE)
        bit = lax.rem(lax.div(head, by), 2)
        going = lax.dynamic_index_in_dim(split, 1 - bit, 2, keepdims=False)
        staying = lax.dynamic_index_in_dim(split, bit, 2, keepdims=False)
        summed = staying + swap(going, "head", by)
        by *= 2
    summed = summed.reshape(blocks, part, STATE)

    pieces = [summed] + [swap(summed, "seq", 2 * by) for by in range(1, levels)]
    sources = jnp.stack([seq ^ (2 * by) for by in range(levels)]).astype(jnp.int32)
    owned = REGIMES // devices

    states, summed = lax.optimization_barrier((states, summed))
    entries, leaves = states_call(
        functools.partial(rounded_kernel, blocks, heads), states, (bf16_states, bf16_states), []
    )
    wide = pl.BlockSpec((BLOCK, 2 * STATE), lambda c, h: (c, h))
    narrow = pl.BlockSpec((BLOCK, 2 * HEAD_DIM), lambda c, h: (c, h))
    states = pl.BlockSpec((1, 2 * HEAD_DIM, STATE), lambda c, h: (c, h, 0))
    query_grad, key_grad, value_grad = pl.pallas_call(
        within_kernel,
        grid=(blocks, heads // 2),
        in_specs=[wide, wide, narrow, narrow, states, states],
        out_specs=[wide, wide, narrow],
        out_shape=(
            shape(*queries.shape, dtype=BF16),
            shape(*keys.shape, dtype=BF16),
            shape(*values.shape, dtype=BF16),
        ),
        compiler_params=PARAMS,
        cost_estimate=pl.CostEstimate(
            flops=blocks * heads * 10 * BLOCK * BLOCK * STATE,
            bytes_accessed=6 << 20,
            transcendentals=0,
        ),
    )(queries, keys, values, out_grad, entries, leaves)
    pieces, query_grad, key_grad, value_grad = lax.optimization_barrier(
        (pieces, query_grad, key_grad, value_grad)
    )

    def regime_sum(device):
        return pl.pallas_call(
            functools.partial(regime_kernel, blocks, owned, len(pieces)),
            in_specs=[SMEM] * 3 + [VMEM] * len(pieces),
            out_specs=VMEM,
            out_shape=shape(owned, part, STATE),
            compiler_params=PARAMS,
        )(regimes, jnp.reshape(device * owned, (1,)).astype(jnp.int32), sources, *pieces)

    arrived_sum = swap(regime_sum(seq ^ 1), "seq", 1)
    regime_grad = pl.pallas_call(
        add_kernel,
        in_specs=[VMEM, VMEM],
        out_specs=VMEM,
        out_shape=shape(owned, part, STATE),
        compiler_params=PARAMS,
    )(regime_sum(seq), arrived_sum)
    return query_grad, key_grad, value_grad, regime_grad


def solution(mesh):
    in_specs = (
        P("seq", "head"),
        P("seq", "head"),
        P("seq", "head"),
        P("seq", "head"),
        P(),
        P("head"),
        P(),
        P(),
    )
    out_specs = (P("seq", "head"), P("seq", "head"), P("seq", "head"), P("seq", "head", None))
    return jax.shard_map(local, mesh=mesh, in_specs=in_specs, out_specs=out_specs, check_vma=False)
```

```python
import functools

import jax
import jax.numpy as jnp
from jax import lax
from jax.experimental import pallas as pl
from jax.experimental.pallas import tpu as pltpu
from jax.sharding import PartitionSpec as P

STATE = 256
HEAD_DIM = 64
REGIMES = 32
BLOCK = 256

F32 = jnp.float32
BF16 = jnp.bfloat16
NN = (((1,), (0,)), ((), ()))
NT = (((1,), (1,)), ((), ()))
TN = (((0,), (0,)), ((), ()))
VMEM = pl.BlockSpec(memory_space=pltpu.VMEM)
SMEM = pl.BlockSpec(memory_space=pltpu.SMEM)
HBM = pl.BlockSpec(memory_space=pltpu.HBM)
PARAMS = pltpu.CompilerParams(vmem_limit_bytes=32 << 20)


def dot(a, b, dims):
    return lax.dot_general(a, b, dims, preferred_element_type=F32)


def halves(x):
    high = x.astype(BF16)
    return high, (x - high.astype(F32)).astype(BF16)


def dot_exact(x, matrix, dims):
    high, low = halves(x)
    return dot(high, matrix, dims) + dot(low, matrix, dims)


def dot_pair(a, b, dims):
    return dot(a[0], b[0], dims) + (dot(a[0], b[1], dims) + dot(a[1], b[0], dims))


def kept_at(documents, block):
    before = documents[jnp.maximum(block - 1, 0)]
    same = jnp.where(documents[block] == before, 1.0, 0.0)
    return jnp.where(block > 0, same, 0.0).astype(F32)


def decay_column(gammas, first, count, power):
    parts = []
    for i in range(count):
        g = gammas[first + i]
        value = g
        for _ in range(power - 1):
            value = value * g
        parts.append(jnp.full((HEAD_DIM, 1), value, F32))
    return jnp.concatenate(parts, axis=0)


def local_kernel(
    blocks, heads, regimes_hbm, documents_hbm, gammas_hbm, transitions, q_hbm, k_hbm, v_hbm, dy_hbm,
    update, source, sent, held, mats,
    q, k, v, dy, regimes, documents, gammas, small_sems, mat_sems, row_sems, wide_sems,
):
    seq = lax.axis_index("seq")
    half = heads * HEAD_DIM // 2
    split = heads * STATE // 2
    small = [
        pltpu.make_async_copy(a, b, small_sems.at[i])
        for i, (a, b) in enumerate(
            ((regimes_hbm, regimes), (documents_hbm, documents), (gammas_hbm, gammas))
        )
    ]
    for copy in small:
        copy.start()
    rows, wide = {}, {}
    for i, (a, b, wide_a, wide_b) in enumerate(((v_hbm, v, k_hbm, k), (dy_hbm, dy, q_hbm, q))):
        for c in range(blocks):
            token = pl.ds(c * BLOCK, BLOCK)
            rows[i, c] = pltpu.make_async_copy(a.at[token], b.at[token], row_sems.at[i, c])
            rows[i, c].start()
            for j in range(2):
                at = (token, pl.ds(j * split, split))
                wide[i, c, j] = pltpu.make_async_copy(
                    wide_a.at[at], wide_b.at[at], wide_sems.at[i, c, j]
                )
                wide[i, c, j].start()
    small[0].wait()
    mat_copies = []
    for c in range(blocks):
        copy = pltpu.make_async_copy(
            transitions.at[regimes[seq * blocks + c]], mats.at[c], mat_sems.at[c]
        )
        copy.start()
        mat_copies.append(copy)
    for i, (out, narrow_in, wide_in) in enumerate(((update, v, k), (source, dy, q))):
        for c in range(blocks):
            token = slice(c * BLOCK, (c + 1) * BLOCK)
            rows[i, c].wait()
            for h in range(heads):
                if h % (heads // 2) == 0:
                    wide[i, c, h // (heads // 2)].wait()
                columns = slice(h * STATE, (h + 1) * STATE)
                narrow = slice(h * HEAD_DIM, (h + 1) * HEAD_DIM)
                out[c, narrow, :] = dot(narrow_in[token, narrow], wide_in[token, columns], TN)
    for copy in small[1:] + mat_copies:
        copy.wait()
    decay = decay_column(gammas, 0, heads, 1)
    state = update[0]
    for c in range(1, blocks):
        factor = kept_at(documents, seq * blocks + c) * decay
        state = update[c] + factor * dot_exact(state, mats[c], NT)
    carried = None
    for c in reversed(range(blocks)):
        total = source[c] if carried is None else source[c] + carried
        factor = kept_at(documents, seq * blocks + c) * decay
        carried = factor * dot_exact(total, mats[c], NN)
    upper = lax.rem(seq, 2) == 1
    for i, value in enumerate((state, carried)):
        first, second = value[:half], value[half:]
        held[i] = jnp.where(upper, second, first)
        sent[i] = jnp.where(upper, first, second)


def maps_kernel(blocks, reach, last_block, regimes, documents, pos, transitions, device_maps, *far):
    seq = pos[0]
    level = lax.div(seq, 2)

    def device_map(device):
        result = None
        for c in range(blocks):
            block = jnp.clip(device * blocks + c, 0, last_block)
            mat = transitions[regimes[block]]
            kept = kept_at(documents, block)
            if result is None:
                result = mat.astype(F32)
            elif c == 1:
                result = dot(mat, result.astype(BF16), NN)
            else:
                high, low = halves(result)
                result = dot(mat, high, NN) + dot(mat, low, NN)
            result = result * kept
        return result

    def pair_map(at):
        low = halves(device_map(at * 2))
        high = halves(device_map(at * 2 + 1))
        return dot_pair(high, low, NN)

    for i in range(2):
        device_maps[i, 0], device_maps[i, 1] = halves(device_map(level * 2 + i))
    if reach > 1:
        far = far[0]
        forward = backward = None
        for distance in range(2, reach + 1):
            behind = pair_map(level - distance + 1)
            ahead = pair_map(level + distance - 1)
            if forward is None:
                forward, backward = behind, ahead
            else:
                forward = dot_pair(halves(forward), halves(behind), NN)
                backward = dot_pair(halves(ahead), halves(backward), NN)
            far[distance - 2, 0, 0], far[distance - 2, 0, 1] = halves(forward)
            far[distance - 2, 1, 0], far[distance - 2, 1, 1] = halves(backward)


def pair_kernel(blocks, heads, routes, pos, gammas, held, arrived, device_maps, *outs):
    seq = pos[0]
    level, upper = lax.div(seq, 2), lax.rem(seq, 2)
    is_upper = upper == 1
    decay = decay_column(gammas, upper * (heads // 2), heads // 2, blocks)
    ends = [jnp.where(is_upper, arrived[0], held[0]), jnp.where(is_upper, held[0], arrived[0])]
    starts = [jnp.where(is_upper, arrived[1], held[1]), jnp.where(is_upper, held[1], arrived[1])]
    low_map = (device_maps[0, 0], device_maps[0, 1])
    high_map = (device_maps[1, 0], device_maps[1, 1])
    forward = ends[1] + decay * dot_pair(halves(ends[0]), high_map, NT)
    backward = starts[0] + decay * dot_pair(halves(starts[1]), low_map, NN)
    for out, (distance, parity) in zip(outs, routes):
        ahead = lax.rem(lax.div(level, distance), 2) == parity
        out[...] = jnp.where(ahead, forward, backward)


def entry_kernel(blocks, heads, reach, routes, pos, gammas, held, arrived, device_maps, *rest):
    count = len(routes)
    received, (own, sent) = rest[:count], rest[-2:]
    far = rest[count] if reach > 1 else None
    seq = pos[0]
    level, upper = lax.div(seq, 2), lax.rem(seq, 2)
    is_upper = upper == 1
    decay = decay_column(gammas, upper * (heads // 2), heads // 2, blocks)
    found = dict(zip(routes, received))
    forward = backward = None
    for distance in range(1, reach + 1):
        even = found[distance, 0][...]
        odd = found[distance, 1][...] if (distance, 1) in found else jnp.zeros_like(even)
        flip = lax.rem(lax.div(level, distance), 2) == 1
        behind = jnp.where(flip, even, odd)
        ahead = jnp.where(flip, odd, even)
        if distance == 1:
            forward, backward = behind, ahead
        else:
            power = decay_column(
                gammas, upper * (heads // 2), heads // 2, 2 * blocks * (distance - 1)
            )
            i = distance - 2
            forward += power * dot_pair(halves(behind), (far[i, 0, 0], far[i, 0, 1]), NT)
            backward += power * dot_pair(halves(ahead), (far[i, 1, 0], far[i, 1, 1]), NN)
    low_map = (device_maps[0, 0], device_maps[0, 1])
    high_map = (device_maps[1, 0], device_maps[1, 1])
    low_end = jnp.where(is_upper, arrived[0], held[0])
    high_start = jnp.where(is_upper, held[1], arrived[1])
    inner_forward = low_end + decay * dot_pair(halves(forward), low_map, NT)
    inner_backward = high_start + decay * dot_pair(halves(backward), high_map, NN)
    own[0] = jnp.where(is_upper, inner_forward, forward)
    own[1] = jnp.where(is_upper, backward, inner_backward)
    sent[0] = jnp.where(is_upper, forward, inner_forward)
    sent[1] = jnp.where(is_upper, inner_backward, backward)


def states_of(blocks, upper, kept, decay, own, arrived, update, source, mats):
    def whole(i):
        first = jnp.where(upper, arrived[i], own[i])
        second = jnp.where(upper, own[i], arrived[i])
        return jnp.concatenate([first, second], axis=0)

    before, carried = whole(0), whole(1)
    befores, entries, leaves, totals = [], [], [None] * blocks, [None] * blocks
    for c in range(blocks):
        befores.append(halves(before))
        high, low = befores[-1]
        entry = (kept[c] * decay) * (dot(high, mats[c], NT) + dot(low, mats[c], NT))
        entries.append(entry)
        before = entry + update[c]
    for c in reversed(range(blocks)):
        leaves[c] = carried
        totals[c] = source[c] + carried
        if c > 0:
            carried = (kept[c] * decay) * dot_exact(totals[c], mats[c], NN)
    return befores, entries, leaves, totals


def terms_kernel(
    blocks, heads, ways, documents, pos, gammas, own, arrived, update, source, mats, held, sent, term
):
    seq, head = pos[0], pos[1]
    decay = decay_column(gammas, 0, heads, 1)
    kept = [kept_at(documents, seq * blocks + c) for c in range(blocks)]
    befores, _, _, totals = states_of(
        blocks, lax.rem(seq, 2) == 1, kept, decay, own, arrived, update, source, mats
    )
    part = STATE // ways
    core = lax.rem(head, 2)
    for c in range(blocks):
        term[...] = dot_pair(halves((kept[c] * decay) * totals[c]), befores[c], TN)
        for i in range(ways // 2):
            held[i, c] = term[pl.ds(pl.multiple_of((2 * i + core) * part, part), part), :]
            sent[i, c] = term[pl.ds(pl.multiple_of((2 * i + 1 - core) * part, part), part), :]


def rounded_kernel(
    blocks, heads, documents, pos, gammas, own, arrived, update, source, mats, entries, leaves
):
    seq = pos[0]
    decay = decay_column(gammas, 0, heads, 1)
    kept = [kept_at(documents, seq * blocks + c) for c in range(blocks)]
    _, entry, leave, _ = states_of(
        blocks, lax.rem(seq, 2) == 1, kept, decay, own, arrived, update, source, mats
    )
    for c in range(blocks):
        entries[c] = entry[c].astype(BF16)
        leaves[c] = leave[c].astype(BF16)


def regime_kernel(blocks, owned, count, regimes, base, sources, *rest):
    pieces, out = rest[:count], rest[count]
    for r in range(owned):
        total = None
        for i in range(count):
            for c in range(blocks):
                match = regimes[sources[i] * blocks + c] == base[0] + r
                value = jnp.where(match, pieces[i][c], 0.0)
                total = value if total is None else total + value
        out[r] = total


def add_kernel(a, b, out):
    out[...] = a[...] + b[...]


def within_kernel(q, k, v, dy, entries, leaves, *rest):
    dq, dk, dv = rest[-3:]
    row = lax.broadcasted_iota(jnp.int32, (BLOCK, BLOCK), 0)
    column = lax.broadcasted_iota(jnp.int32, (BLOCK, BLOCK), 1)
    lower, upper = row >= column, row <= column
    for h in range(v.shape[1] // HEAD_DIM):
        wide = slice(h * STATE, (h + 1) * STATE)
        narrow = slice(h * HEAD_DIM, (h + 1) * HEAD_DIM)
        qh, kh, vh, gh = q[:, wide], k[:, wide], v[:, narrow], dy[:, narrow]
        entry, leave = entries[0, narrow, :], leaves[0, narrow, :]
        probs_t = jnp.where(upper, dot(kh, qh, NT), 0.0).astype(BF16)
        dscore = jnp.where(lower, dot(gh, vh, NT), 0.0).astype(BF16)
        dscore_t = jnp.where(upper, dot(vh, gh, NT), 0.0).astype(BF16)
        dq[:, wide] = (dot(gh, entry, NN) + dot(dscore, kh, NN)).astype(BF16)
        dk[:, wide] = (dot(vh, leave, NN) + dot(dscore_t, qh, NN)).astype(BF16)
        dv[:, narrow] = (dot(kh, leave, NT) + dot(probs_t, gh, NN)).astype(BF16)


def swap(x, axis, by):
    count = lax.axis_size(axis)
    return lax.ppermute(x, axis, [(i, i ^ by) for i in range(count)])


def level_route(x, distance, parity):
    levels = lax.axis_size("seq") // 2
    pairs = []
    for low in range(levels - distance):
        if (low // distance) % 2 == parity:
            for side in range(2):
                a, b = 2 * low + side, 2 * (low + distance) + side
                pairs += [(a, b), (b, a)]
    return lax.ppermute(x, "seq", pairs)


def routes_up_to(reach, levels):
    return [
        (distance, parity)
        for distance in range(1, reach + 1)
        for parity in range(2)
        if any((low // distance) % 2 == parity for low in range(levels - distance))
    ]


def local(queries, keys, values, out_grad, transitions, gammas, regimes, documents):
    tokens_dev = queries.shape[0]
    heads = gammas.shape[0]
    blocks = tokens_dev // BLOCK
    all_blocks = documents.shape[0]
    devices, ways = lax.axis_size("seq"), lax.axis_size("head")
    levels = devices // 2
    rows = heads * HEAD_DIM
    half = rows // 2
    reach = min(levels - 1, -(-(all_blocks // 2 - 1) // (2 * blocks)))
    routes = routes_up_to(reach, levels)[::-1]
    seq, head = lax.axis_index("seq"), lax.axis_index("head")
    pos = jnp.stack([seq, head]).astype(jnp.int32)

    def shape(*dims, dtype=F32):
        return jax.ShapeDtypeStruct(dims, dtype)

    state_shape = shape(blocks, rows, STATE)
    half_shape = shape(2, half, STATE)
    outs = (state_shape, state_shape, half_shape, half_shape)
    def in_hbm(x):
        return pltpu.with_memory_space_constraint(x, pltpu.HBM)

    def in_vmem(x):
        return pltpu.VMEM(x.shape, x.dtype)

    mat_shape = shape(blocks, STATE, STATE, dtype=BF16)
    inputs = (queries, keys, values, out_grad)
    update, source, sent, held, mats = pl.pallas_call(
        functools.partial(local_kernel, blocks, heads),
        in_specs=[HBM] * 8,
        out_specs=(VMEM,) * 5,
        out_shape=tuple(in_vmem(x) for x in outs + (mat_shape,)),
        scratch_shapes=[in_vmem(x) for x in inputs]
        + [
            pltpu.SMEM(regimes.shape, jnp.int32),
            pltpu.SMEM(documents.shape, jnp.int32),
            pltpu.SMEM(gammas.shape, F32),
            pltpu.SemaphoreType.DMA((3,)),
            pltpu.SemaphoreType.DMA((blocks,)),
            pltpu.SemaphoreType.DMA((2, blocks)),
            pltpu.SemaphoreType.DMA((2, blocks, 2)),
        ],
        compiler_params=PARAMS,
    )(
        *[in_hbm(x) for x in (regimes, documents, gammas, transitions) + inputs]
    )

    arrived = swap(sent, "seq", 1)
    map_shapes = (shape(2, 2, STATE, STATE, dtype=BF16),)
    if reach > 1:
        map_shapes += (shape(reach - 1, 2, 2, STATE, STATE, dtype=BF16),)
    maps = pl.pallas_call(
        functools.partial(maps_kernel, blocks, reach, all_blocks - 1),
        in_specs=[SMEM, SMEM, SMEM, VMEM],
        out_specs=(VMEM,) * len(map_shapes),
        out_shape=map_shapes,
        compiler_params=PARAMS,
    )(regimes, documents, pos, transitions)

    trades = pl.pallas_call(
        functools.partial(pair_kernel, blocks, heads, routes),
        in_specs=[SMEM, SMEM, VMEM, VMEM, VMEM],
        out_specs=(VMEM,) * len(routes),
        out_shape=(shape(half, STATE),) * len(routes),
        compiler_params=PARAMS,
    )(pos, gammas, held, arrived, maps[0])
    received = [level_route(x, *route) for x, route in zip(trades, routes)]

    own, sent_entry = pl.pallas_call(
        functools.partial(entry_kernel, blocks, heads, reach, routes),
        in_specs=[SMEM, SMEM] + [VMEM] * (3 + len(received) + len(maps) - 1),
        out_specs=(VMEM, VMEM),
        out_shape=(half_shape, half_shape),
        compiler_params=PARAMS,
    )(pos, gammas, held, arrived, maps[0], *received, *maps[1:])
    arrived_entry = swap(sent_entry, "seq", 1)

    part = STATE // ways
    part_shape = shape(ways // 2, blocks, part, STATE)
    bf16_states = shape(blocks, rows, STATE, dtype=BF16)
    states = (own, arrived_entry, update, source, mats)

    def states_call(kernel, states, outs, scratch):
        return pl.pallas_call(
            kernel,
            in_specs=[SMEM] * 3 + [VMEM] * len(states),
            out_specs=(VMEM,) * len(outs),
            out_shape=outs,
            scratch_shapes=scratch,
            compiler_params=PARAMS,
        )(documents, pos, gammas, *states)

    held_term, sent_term = states_call(
        functools.partial(terms_kernel, blocks, heads, ways),
        states,
        (part_shape, part_shape),
        [pltpu.VMEM((STATE, STATE), F32)],
    )

    summed = held_term + swap(sent_term, "head", 1)
    states, summed = lax.optimization_barrier((states, summed))
    entries, leaves = states_call(
        functools.partial(rounded_kernel, blocks, heads), states, (bf16_states, bf16_states), []
    )
    by = 2
    while by < ways:
        split = summed.reshape(-1, 2, blocks, part, STATE)
        bit = lax.rem(lax.div(head, by), 2)
        going = lax.dynamic_index_in_dim(split, 1 - bit, 1, keepdims=False)
        staying = lax.dynamic_index_in_dim(split, bit, 1, keepdims=False)
        arrived_part = swap(going, "head", by)
        arrived_part, entries, leaves = lax.optimization_barrier((arrived_part, entries, leaves))
        summed = staying + arrived_part
        by *= 2
    summed = summed.reshape(blocks, part, STATE)
    summed, entries, leaves = lax.optimization_barrier((summed, entries, leaves))

    def output_call(c, entries, leaves, before):
        wide = pl.BlockSpec((BLOCK, 2 * STATE), lambda h: (c, h))
        narrow = pl.BlockSpec((BLOCK, 2 * HEAD_DIM), lambda h: (c, h))
        state = pl.BlockSpec((1, 2 * HEAD_DIM, STATE), lambda h: (c, h, 0))
        return pl.pallas_call(
            within_kernel,
            grid=(heads // 2,),
            in_specs=[wide, wide, narrow, narrow, state, state] + [HBM] * len(before),
            out_specs=[wide, wide, narrow],
            out_shape=[shape(*x.shape, dtype=BF16) for x in inputs[:3]],
            input_output_aliases={6 + i: i for i in range(len(before))},
            compiler_params=PARAMS,
            cost_estimate=pl.CostEstimate(
                flops=20 * heads * BLOCK * BLOCK * STATE,
                bytes_accessed=3 << 20,
                transcendentals=0,
            ),
        )(*[in_hbm(x) for x in inputs], entries, leaves, *before)

    pieces, sources, by = [summed], [seq], devices // 2
    direct = [swap(summed, "seq", 1 << i) for i in range(1, by.bit_length())][::-1]
    grads = output_call(0, entries, leaves, ())
    direct, grads = lax.optimization_barrier((direct, grads))
    while by > 1:
        pieces += [direct[0]] + [swap(x, "seq", by) for x in pieces[1:]]
        sources += [x ^ by for x in sources]
        direct, by = direct[1:], by // 2
    sources = jnp.stack(sources).astype(jnp.int32)
    owned = REGIMES // devices

    def regime_sum(device):
        return pl.pallas_call(
            functools.partial(regime_kernel, blocks, owned, len(pieces)),
            in_specs=[SMEM] * 3 + [VMEM] * len(pieces),
            out_specs=VMEM,
            out_shape=shape(owned, part, STATE),
            compiler_params=PARAMS,
        )(regimes, jnp.reshape(device * owned, (1,)).astype(jnp.int32), sources, *pieces)

    sent_sum = regime_sum(seq ^ 1)
    sent_sum, grads = lax.optimization_barrier((sent_sum, grads))
    arrived_sum = swap(sent_sum, "seq", 1)
    for c in range(1, blocks):
        grads = output_call(c, entries, leaves, grads)
    own_sum = regime_sum(seq)
    arrived_sum, own_sum, grads = lax.optimization_barrier((arrived_sum, own_sum, grads))
    regime_grad = pl.pallas_call(
        add_kernel,
        in_specs=[VMEM, VMEM],
        out_specs=VMEM,
        out_shape=shape(owned, part, STATE),
        compiler_params=PARAMS,
    )(own_sum, arrived_sum)
    return (*grads, regime_grad)


def solution(mesh):
    in_specs = (
        P("seq", "head"),
        P("seq", "head"),
        P("seq", "head"),
        P("seq", "head"),
        P(),
        P("head"),
        P(),
        P(),
    )
    out_specs = (P("seq", "head"), P("seq", "head"), P("seq", "head"), P("seq", "head", None))
    return jax.shard_map(local, mesh=mesh, in_specs=in_specs, out_specs=out_specs, check_vma=False)
```

```python
import functools

import jax
import jax.numpy as jnp
from jax import lax
from jax.experimental import pallas as pl
from jax.experimental.pallas import tpu as pltpu
from jax.sharding import PartitionSpec as P

STATE = 256
HEAD_DIM = 64
REGIMES = 32
BLOCK = 256

F32 = jnp.float32
BF16 = jnp.bfloat16
NN = (((1,), (0,)), ((), ()))
NT = (((1,), (1,)), ((), ()))
TN = (((0,), (0,)), ((), ()))
VMEM = pl.BlockSpec(memory_space=pltpu.VMEM)
SMEM = pl.BlockSpec(memory_space=pltpu.SMEM)
HBM = pl.BlockSpec(memory_space=pltpu.HBM)
PARAMS = pltpu.CompilerParams(vmem_limit_bytes=32 << 20)


def dot(a, b, dims):
    return lax.dot_general(a, b, dims, preferred_element_type=F32)


def halves(x):
    high = x.astype(BF16)
    return high, (x - high.astype(F32)).astype(BF16)


def dot_exact(x, matrix, dims):
    high, low = halves(x)
    return dot(high, matrix, dims) + dot(low, matrix, dims)


def dot_pair(a, b, dims):
    return dot(a[0], b[0], dims) + (dot(a[0], b[1], dims) + dot(a[1], b[0], dims))


def kept_at(documents, block):
    before = documents[jnp.maximum(block - 1, 0)]
    same = jnp.where(documents[block] == before, 1.0, 0.0)
    return jnp.where(block > 0, same, 0.0).astype(F32)


def decay_column(gammas, first, count, power):
    parts = []
    for i in range(count):
        g = gammas[first + i]
        value = g
        for _ in range(power - 1):
            value = value * g
        parts.append(jnp.full((HEAD_DIM, 1), value, F32))
    return jnp.concatenate(parts, axis=0)


def local_kernel(
    blocks, heads, regimes_hbm, documents_hbm, gammas_hbm, transitions, q_hbm, k_hbm, v_hbm, dy_hbm,
    update, source, sent, held, mats,
    q, k, v, dy, regimes, documents, gammas, small_sems, mat_sems, row_sems, wide_sems,
):
    seq = lax.axis_index("seq")
    half = heads * HEAD_DIM // 2
    small = [
        pltpu.make_async_copy(a, b, small_sems.at[i])
        for i, (a, b) in enumerate(
            ((regimes_hbm, regimes), (documents_hbm, documents), (gammas_hbm, gammas))
        )
    ]
    for copy in small:
        copy.start()
    rows, wide = [], {}
    for i, (a, b) in enumerate(((v_hbm, v), (dy_hbm, dy))):
        rows.append(pltpu.make_async_copy(a, b, row_sems.at[i]))
    rows[0].start()
    for i, (a, b) in enumerate(((k_hbm, k), (q_hbm, q))):
        wide[i] = pltpu.make_async_copy(a, b, wide_sems.at[i, 0])
        wide[i].start()
        if i == 0:
            rows[1].start()
    small[0].wait()
    mat_copies = []
    for c in range(blocks):
        copy = pltpu.make_async_copy(
            transitions.at[regimes[seq * blocks + c]], mats.at[c], mat_sems.at[c]
        )
        copy.start()
        mat_copies.append(copy)
    def products(i, c, out, narrow_in, wide_in):
        token = slice(c * BLOCK, (c + 1) * BLOCK)
        if c == (0, blocks - 1)[i]:
            rows[i].wait()
        flipped = narrow_in[token, :].T
        if c == (0, blocks - 1)[i]:
            wide[i].wait()
        for h in range(heads):
            columns = slice(h * STATE, (h + 1) * STATE)
            narrow = slice(h * HEAD_DIM, (h + 1) * HEAD_DIM)
            out[c, narrow, :] = dot(flipped[narrow], wide_in[token, columns], NN)

    for c in range(blocks):
        products(0, c, update, v, k)
    for copy in small[1:] + mat_copies:
        copy.wait()
    decay = decay_column(gammas, 0, heads, 1)
    factors = [kept_at(documents, seq * blocks + c) * decay for c in range(blocks)]
    state = update[0]
    for c in range(1, blocks):
        state = update[c] + factors[c] * dot_exact(state, mats[c], NT)
    carried = None
    for c in reversed(range(blocks)):
        products(1, c, source, dy, q)
        total = source[c] if carried is None else source[c] + carried
        carried = factors[c] * dot_exact(total, mats[c], NN)
    upper = lax.rem(seq, 2) == 1
    for i, value in enumerate((state, carried)):
        first, second = value[:half], value[half:]
        held[i] = jnp.where(upper, second, first)
        sent[i] = jnp.where(upper, first, second)


def maps_kernel(
    blocks, heads, reach, masks, regimes, documents, gammas, transitions,
    device_maps, powers, factors, weights, *rest,
):
    seq = lax.axis_index("seq")
    level = lax.div(seq, 2)
    last_block = documents.shape[0] - 1
    far, (mats, mat_sems) = rest[:-2], rest[-2:]
    first = (level - reach + 1) * 2 * blocks
    copies = []
    for i in range(mats.shape[0]):
        block = jnp.clip(first + i, 0, last_block)
        copies.append(
            pltpu.make_async_copy(transitions.at[regimes[block]], mats.at[i], mat_sems.at[i])
        )
        copies[-1].start()
    for i in range(reach):
        powers[i] = decay_column(gammas, 0, heads, blocks * max(1, 2 * i))
    decay = decay_column(gammas, 0, heads, 1)
    for c in range(blocks):
        factors[c] = kept_at(documents, seq * blocks + c) * decay
    owned, count = weights.shape[1:3]
    for i, mask in enumerate(masks):
        for c in range(blocks):
            regime = regimes[(seq ^ mask) * blocks + c]
            for j in range(2):
                for r in range(owned):
                    match = regime == (seq ^ (1 - j)) * owned + r
                    weights[j, r, i * blocks + c : i * blocks + c + 1, :] = jnp.full(
                        (1, STATE), jnp.where(match, 1.0, 0.0).astype(F32)
                    )

    for copy in copies:
        copy.wait()

    def device_map(device):
        result = None
        for c in range(blocks):
            block = jnp.clip(device * blocks + c, 0, last_block)
            mat = mats[device * blocks + c - first]
            kept = kept_at(documents, block)
            if result is None:
                result = mat.astype(F32)
            elif c == 1:
                result = dot(mat, result.astype(BF16), NN)
            else:
                high, low = halves(result)
                result = dot(mat, high, NN) + dot(mat, low, NN)
            result = result * kept
        return result

    def pair_map(at):
        low = halves(device_map(at * 2))
        high = halves(device_map(at * 2 + 1))
        return dot_pair(high, low, NN)

    for i in range(2):
        device_maps[i, 0], device_maps[i, 1] = halves(device_map(level * 2 + i))
    if reach > 1:
        far = far[0]
        forward = backward = None
        for distance in range(2, reach + 1):
            behind = pair_map(level - distance + 1)
            ahead = pair_map(level + distance - 1)
            if forward is None:
                forward, backward = behind, ahead
            else:
                forward = dot_pair(halves(forward), halves(behind), NN)
                backward = dot_pair(halves(ahead), halves(backward), NN)
            far[distance - 2, 0, 0], far[distance - 2, 0, 1] = halves(forward)
            far[distance - 2, 1, 0], far[distance - 2, 1, 1] = halves(backward)


def half_rows(columns, i, upper):
    half = columns.shape[1] // 2
    return columns[i, pl.ds(pl.multiple_of(upper * half, half), half), :]


def pair_kernel(routes, powers, held, arrived, device_maps, *outs):
    seq = lax.axis_index("seq")
    level, upper = lax.div(seq, 2), lax.rem(seq, 2)
    is_upper = upper == 1
    decay = half_rows(powers, 0, upper)
    ends = [jnp.where(is_upper, arrived[0], held[0]), jnp.where(is_upper, held[0], arrived[0])]
    starts = [jnp.where(is_upper, arrived[1], held[1]), jnp.where(is_upper, held[1], arrived[1])]
    low_map = (device_maps[0, 0], device_maps[0, 1])
    high_map = (device_maps[1, 0], device_maps[1, 1])
    forward = ends[1] + decay * dot_pair(halves(ends[0]), high_map, NT)
    backward = starts[0] + decay * dot_pair(halves(starts[1]), low_map, NN)
    for out, (distance, parity) in zip(outs, routes):
        ahead = lax.rem(lax.div(level, distance), 2) == parity
        out[...] = jnp.where(ahead, forward, backward)


def entry_kernel(reach, routes, powers, held, arrived, device_maps, *rest):
    count = len(routes)
    received, (own, sent) = rest[:count], rest[-2:]
    far = rest[count] if reach > 1 else None
    seq = lax.axis_index("seq")
    level, upper = lax.div(seq, 2), lax.rem(seq, 2)
    is_upper = upper == 1
    decay = half_rows(powers, 0, upper)
    found = dict(zip(routes, received))
    forward = backward = None
    for distance in range(1, reach + 1):
        even = found[distance, 0][...]
        odd = found[distance, 1][...] if (distance, 1) in found else jnp.zeros_like(even)
        flip = lax.rem(lax.div(level, distance), 2) == 1
        behind = jnp.where(flip, even, odd)
        ahead = jnp.where(flip, odd, even)
        if distance == 1:
            forward, backward = behind, ahead
        else:
            power = half_rows(powers, distance - 1, upper)
            i = distance - 2
            forward += power * dot_pair(halves(behind), (far[i, 0, 0], far[i, 0, 1]), NT)
            backward += power * dot_pair(halves(ahead), (far[i, 1, 0], far[i, 1, 1]), NN)
    low_map = (device_maps[0, 0], device_maps[0, 1])
    high_map = (device_maps[1, 0], device_maps[1, 1])
    low_end = jnp.where(is_upper, arrived[0], held[0])
    high_start = jnp.where(is_upper, held[1], arrived[1])
    inner_forward = low_end + decay * dot_pair(halves(forward), low_map, NT)
    inner_backward = high_start + decay * dot_pair(halves(backward), high_map, NN)
    own[0] = jnp.where(is_upper, inner_forward, forward)
    own[1] = jnp.where(is_upper, backward, inner_backward)
    sent[0] = jnp.where(is_upper, forward, inner_forward)
    sent[1] = jnp.where(is_upper, inner_backward, backward)


def states_of(blocks, factors, own, arrived, update, source, mats):
    upper = lax.rem(lax.axis_index("seq"), 2) == 1

    def whole(i):
        first = jnp.where(upper, arrived[i], own[i])
        second = jnp.where(upper, own[i], arrived[i])
        return jnp.concatenate([first, second], axis=0)

    before, carried = whole(0), whole(1)
    befores, entries, leaves, totals = [], [], [None] * blocks, [None] * blocks
    for c in range(blocks):
        befores.append(halves(before))
        high, low = befores[-1]
        entry = factors[c] * (dot(high, mats[c], NT) + dot(low, mats[c], NT))
        entries.append(entry)
        before = entry + update[c]
    for c in reversed(range(blocks)):
        leaves[c] = carried
        totals[c] = source[c] + carried
        if c > 0:
            carried = factors[c] * dot_exact(totals[c], mats[c], NN)
    return befores, entries, leaves, totals


def terms_kernel(blocks, ways, factors, own, arrived, update, source, mats, held, sent, term):
    head = lax.axis_index("head")
    befores, _, _, totals = states_of(blocks, factors, own, arrived, update, source, mats)
    part = STATE // ways
    core = lax.rem(head, 2)
    for c in range(blocks):
        term[...] = dot_pair(halves(factors[c] * totals[c]), befores[c], TN)
        for i in range(ways // 2):
            held[i, c] = term[pl.ds(pl.multiple_of((2 * i + core) * part, part), part), :]
            sent[i, c] = term[pl.ds(pl.multiple_of((2 * i + 1 - core) * part, part), part), :]


def rounded_kernel(blocks, factors, own, arrived, update, source, mats, entries, leaves):
    _, entry, leave, _ = states_of(blocks, factors, own, arrived, update, source, mats)
    for c in range(blocks):
        entries[c] = entry[c].astype(BF16)
        leaves[c] = leave[c].astype(BF16)


def regime_kernel(owner, weights, *rest):
    pieces, out = rest[:-1], rest[-1]
    blocks = pieces[0].shape[0]
    for r in range(out.shape[0]):
        total = None
        for i, piece in enumerate(pieces):
            for c in range(blocks):
                at = i * blocks + c
                value = weights[owner, r, at : at + 1, :] * piece[c]
                total = value if total is None else total + value
        out[r] = total


def add_kernel(a, b, out):
    out[...] = a[...] + b[...]


def within_kernel(q, k, v, dy, entries, leaves, *rest):
    dq, dk, dv = rest[-3:]
    row = lax.broadcasted_iota(jnp.int32, (BLOCK, BLOCK), 0)
    column = lax.broadcasted_iota(jnp.int32, (BLOCK, BLOCK), 1)
    lower, upper = row >= column, row <= column
    for h in range(v.shape[1] // HEAD_DIM):
        wide = slice(h * STATE, (h + 1) * STATE)
        narrow = slice(h * HEAD_DIM, (h + 1) * HEAD_DIM)
        qh, kh, vh, gh = q[:, wide], k[:, wide], v[:, narrow], dy[:, narrow]
        entry, leave = entries[0, narrow, :], leaves[0, narrow, :]
        probs_t = jnp.where(upper, dot(kh, qh, NT), 0.0).astype(BF16)
        dscore = jnp.where(lower, dot(gh, vh, NT), 0.0).astype(BF16)
        dscore_t = jnp.where(upper, dot(vh, gh, NT), 0.0).astype(BF16)
        dq[:, wide] = (dot(gh, entry, NN) + dot(dscore, kh, NN)).astype(BF16)
        dk[:, wide] = (dot(vh, leave, NN) + dot(dscore_t, qh, NN)).astype(BF16)
        dv[:, narrow] = (dot(kh, leave, NT) + dot(probs_t, gh, NN)).astype(BF16)


def swap(x, axis, by):
    count = lax.axis_size(axis)
    return lax.ppermute(x, axis, [(i, i ^ by) for i in range(count)])


def level_route(x, distance, parity):
    levels = lax.axis_size("seq") // 2
    pairs = []
    for low in range(levels - distance):
        if (low // distance) % 2 == parity:
            for side in range(2):
                a, b = 2 * low + side, 2 * (low + distance) + side
                pairs += [(a, b), (b, a)]
    return lax.ppermute(x, "seq", pairs)


def routes_up_to(reach, levels):
    return [
        (distance, parity)
        for distance in range(1, reach + 1)
        for parity in range(2)
        if any((low // distance) % 2 == parity for low in range(levels - distance))
    ]


def local(queries, keys, values, out_grad, transitions, gammas, regimes, documents):
    tokens_dev = queries.shape[0]
    heads = gammas.shape[0]
    blocks = tokens_dev // BLOCK
    all_blocks = documents.shape[0]
    devices, ways = lax.axis_size("seq"), lax.axis_size("head")
    levels = devices // 2
    rows = heads * HEAD_DIM
    half = rows // 2
    reach = min(levels - 1, -(-(all_blocks // 2 - 1) // (2 * blocks)))
    routes = routes_up_to(reach, levels)[::-1]
    head = lax.axis_index("head")
    owned, part = REGIMES // devices, STATE // ways
    masks, by = [0], devices // 2
    while by > 1:
        masks += [x ^ by for x in masks]
        by //= 2

    def shape(*dims, dtype=F32):
        return jax.ShapeDtypeStruct(dims, dtype)

    state_shape = shape(blocks, rows, STATE)
    half_shape = shape(2, half, STATE)
    outs = (state_shape, state_shape, half_shape, half_shape)
    def in_hbm(x):
        return pltpu.with_memory_space_constraint(x, pltpu.HBM)

    def in_vmem(x):
        return pltpu.VMEM(x.shape, x.dtype)

    mat_shape = shape(blocks, STATE, STATE, dtype=BF16)
    inputs = (queries, keys, values, out_grad)
    update, source, sent, held, mats = pl.pallas_call(
        functools.partial(local_kernel, blocks, heads),
        in_specs=[HBM] * 8,
        out_specs=(VMEM,) * 5,
        out_shape=tuple(in_vmem(x) for x in outs + (mat_shape,)),
        scratch_shapes=[in_vmem(x) for x in inputs]
        + [
            pltpu.SMEM(regimes.shape, jnp.int32),
            pltpu.SMEM(documents.shape, jnp.int32),
            pltpu.SMEM(gammas.shape, F32),
            pltpu.SemaphoreType.DMA((3,)),
            pltpu.SemaphoreType.DMA((blocks,)),
            pltpu.SemaphoreType.DMA((2,)),
            pltpu.SemaphoreType.DMA((2, blocks)),
        ],
        compiler_params=PARAMS,
    )(
        *[in_hbm(x) for x in (regimes, documents, gammas, transitions) + inputs]
    )

    arrived = swap(sent, "seq", 1)
    map_shapes = (
        shape(2, 2, STATE, STATE, dtype=BF16),
        shape(reach, rows, 1),
        shape(blocks, rows, 1),
        shape(2, owned, len(masks) * blocks, STATE),
    )
    if reach > 1:
        map_shapes += (shape(reach - 1, 2, 2, STATE, STATE, dtype=BF16),)
    needed = (2 * reach - 1) * 2 * blocks
    device_maps, powers, factors, weights, *far = pl.pallas_call(
        functools.partial(maps_kernel, blocks, heads, reach, masks),
        in_specs=[SMEM, SMEM, SMEM, HBM],
        out_specs=(VMEM,) * len(map_shapes),
        out_shape=map_shapes,
        scratch_shapes=[
            pltpu.VMEM((needed, STATE, STATE), BF16),
            pltpu.SemaphoreType.DMA((needed,)),
        ],
        compiler_params=PARAMS,
    )(regimes, documents, gammas, in_hbm(transitions))

    trades = pl.pallas_call(
        functools.partial(pair_kernel, routes),
        in_specs=[VMEM] * 4,
        out_specs=(VMEM,) * len(routes),
        out_shape=(shape(half, STATE),) * len(routes),
        compiler_params=PARAMS,
    )(powers, held, arrived, device_maps)
    received = [level_route(x, *route) for x, route in zip(trades, routes)]

    own, sent_entry = pl.pallas_call(
        functools.partial(entry_kernel, reach, routes),
        in_specs=[VMEM] * (4 + len(received) + len(far)),
        out_specs=(VMEM, VMEM),
        out_shape=(half_shape, half_shape),
        compiler_params=PARAMS,
    )(powers, held, arrived, device_maps, *received, *far)
    arrived_entry = swap(sent_entry, "seq", 1)

    part_shape = shape(ways // 2, blocks, part, STATE)
    bf16_states = shape(blocks, rows, STATE, dtype=BF16)
    states = (factors, own, arrived_entry, update, source, mats)

    def states_call(kernel, states, outs, scratch):
        return pl.pallas_call(
            kernel,
            in_specs=[VMEM] * len(states),
            out_specs=(VMEM,) * len(outs),
            out_shape=outs,
            scratch_shapes=scratch,
            compiler_params=PARAMS,
        )(*states)

    held_term, sent_term = states_call(
        functools.partial(terms_kernel, blocks, ways),
        states,
        (part_shape, part_shape),
        [pltpu.VMEM((STATE, STATE), F32)],
    )

    def output_call(c, entries, leaves, before):
        wide = pl.BlockSpec((BLOCK, 2 * STATE), lambda h: (c, h))
        narrow = pl.BlockSpec((BLOCK, 2 * HEAD_DIM), lambda h: (c, h))
        state = pl.BlockSpec((1, 2 * HEAD_DIM, STATE), lambda h: (c, h, 0))
        return pl.pallas_call(
            within_kernel,
            grid=(heads // 2,),
            in_specs=[wide, wide, narrow, narrow, state, state] + [HBM] * len(before),
            out_specs=[wide, wide, narrow],
            out_shape=[shape(*x.shape, dtype=BF16) for x in inputs[:3]],
            input_output_aliases={6 + i: i for i in range(len(before))},
            compiler_params=PARAMS,
            cost_estimate=pl.CostEstimate(
                flops=20 * heads * BLOCK * BLOCK * STATE,
                bytes_accessed=3 << 20,
                transcendentals=0,
            ),
        )(*[in_hbm(x) for x in inputs], entries, leaves, *before)

    sent_term, states = lax.optimization_barrier((sent_term, states))
    arrived_term = swap(sent_term, "head", 1)
    entries, leaves = states_call(
        functools.partial(rounded_kernel, blocks), states, (bf16_states, bf16_states), []
    )
    arrived_term, entries, leaves = lax.optimization_barrier((arrived_term, entries, leaves))
    summed = held_term + arrived_term
    by, grads = 2, ()
    while by < ways:
        split = summed.reshape(-1, 2, blocks, part, STATE)
        bit = lax.rem(lax.div(head, by), 2)
        going = lax.dynamic_index_in_dim(split, 1 - bit, 1, keepdims=False)
        staying = lax.dynamic_index_in_dim(split, bit, 1, keepdims=False)
        going, entries, leaves = lax.optimization_barrier((going, entries, leaves))
        arrived_part = swap(going, "head", by)
        if not grads:
            grads = output_call(0, entries, leaves, ())
            arrived_part, grads = lax.optimization_barrier((arrived_part, grads))
        summed = staying + arrived_part
        by *= 2
    summed = summed.reshape(blocks, part, STATE)

    pieces, by = [summed], devices // 2
    direct = [swap(summed, "seq", 1 << i) for i in range(1, by.bit_length())][::-1]
    direct = lax.optimization_barrier(direct)
    while by > 1:
        pieces += [direct[0]] + [swap(x, "seq", by) for x in pieces[1:]]
        direct, by = direct[1:], by // 2

    def regime_sum(owner):
        return pl.pallas_call(
            functools.partial(regime_kernel, owner),
            in_specs=[VMEM] * (1 + len(pieces)),
            out_specs=VMEM,
            out_shape=shape(owned, part, STATE),
            compiler_params=PARAMS,
        )(weights, *pieces)

    sent_sum = regime_sum(0)
    sent_sum, grads = lax.optimization_barrier((sent_sum, grads))
    arrived_sum = swap(sent_sum, "seq", 1)
    for c in range(1, blocks):
        grads = output_call(c, entries, leaves, grads)
    own_sum = regime_sum(1)
    arrived_sum, own_sum, grads = lax.optimization_barrier((arrived_sum, own_sum, grads))
    regime_grad = pl.pallas_call(
        add_kernel,
        in_specs=[VMEM, VMEM],
        out_specs=VMEM,
        out_shape=shape(owned, part, STATE),
        compiler_params=PARAMS,
    )(own_sum, arrived_sum)
    return (*grads, regime_grad)


def solution(mesh):
    in_specs = (
        P("seq", "head"),
        P("seq", "head"),
        P("seq", "head"),
        P("seq", "head"),
        P(),
        P("head"),
        P(),
        P(),
    )
    out_specs = (P("seq", "head"), P("seq", "head"), P("seq", "head"), P("seq", "head", None))
    return jax.shard_map(local, mesh=mesh, in_specs=in_specs, out_specs=out_specs, check_vma=False)
```

```python
import functools

import jax
import jax.numpy as jnp
from jax import lax
from jax.experimental import pallas as pl
from jax.experimental.pallas import tpu as pltpu
from jax.sharding import PartitionSpec as P

STATE = 256
HEAD_DIM = 64
REGIMES = 32
BLOCK = 256

F32 = jnp.float32
BF16 = jnp.bfloat16
NN = (((1,), (0,)), ((), ()))
NT = (((1,), (1,)), ((), ()))
TN = (((0,), (0,)), ((), ()))
VMEM = pl.BlockSpec(memory_space=pltpu.VMEM)
SMEM = pl.BlockSpec(memory_space=pltpu.SMEM)
HBM = pl.BlockSpec(memory_space=pltpu.HBM)
PARAMS = pltpu.CompilerParams(vmem_limit_bytes=32 << 20)


def dot(a, b, dims):
    return lax.dot_general(a, b, dims, preferred_element_type=F32)


def halves(x):
    high = x.astype(BF16)
    return high, (x - high.astype(F32)).astype(BF16)


def dot_exact(x, matrix, dims):
    high, low = halves(x)
    return dot(high, matrix, dims) + dot(low, matrix, dims)


def dot_pair(a, b, dims):
    return dot(a[0], b[0], dims) + (dot(a[0], b[1], dims) + dot(a[1], b[0], dims))


def kept_at(documents, block):
    before = documents[jnp.maximum(block - 1, 0)]
    same = jnp.where(documents[block] == before, 1.0, 0.0)
    return jnp.where(block > 0, same, 0.0).astype(F32)


def decay_column(gammas, first, count, power):
    parts = []
    for i in range(count):
        g = gammas[first + i]
        value = g
        for _ in range(power - 1):
            value = value * g
        parts.append(jnp.full((HEAD_DIM, 1), value, F32))
    return jnp.concatenate(parts, axis=0)


def local_kernel(
    blocks, heads, regimes_hbm, documents_hbm, gammas_hbm, transitions, q_hbm, k_hbm, v_hbm, dy_hbm,
    update, source, sent, held, mats,
    q, k, v, dy, regimes, documents, gammas, small_sems, mat_sems, row_sems, wide_sems,
):
    seq = lax.axis_index("seq")
    half = heads * HEAD_DIM // 2
    small = [
        pltpu.make_async_copy(a, b, small_sems.at[i])
        for i, (a, b) in enumerate(
            ((regimes_hbm, regimes), (documents_hbm, documents), (gammas_hbm, gammas))
        )
    ]
    for copy in small:
        copy.start()
    rows, wide = [], {}
    for i, (a, b) in enumerate(((v_hbm, v), (dy_hbm, dy))):
        rows.append(pltpu.make_async_copy(a, b, row_sems.at[i]))
    rows[0].start()
    for i, (a, b) in enumerate(((k_hbm, k), (q_hbm, q))):
        wide[i] = pltpu.make_async_copy(a, b, wide_sems.at[i, 0])
        wide[i].start()
        if i == 0:
            rows[1].start()
    small[0].wait()
    mat_copies = []
    for c in range(blocks):
        copy = pltpu.make_async_copy(
            transitions.at[regimes[seq * blocks + c]], mats.at[c], mat_sems.at[c]
        )
        copy.start()
        mat_copies.append(copy)
    def products(i, c, out, narrow_in, wide_in):
        token = slice(c * BLOCK, (c + 1) * BLOCK)
        if c == (0, blocks - 1)[i]:
            rows[i].wait()
        flipped = narrow_in[token, :].T
        if c == (0, blocks - 1)[i]:
            wide[i].wait()
        for h in range(heads):
            columns = slice(h * STATE, (h + 1) * STATE)
            narrow = slice(h * HEAD_DIM, (h + 1) * HEAD_DIM)
            out[c, narrow, :] = dot(flipped[narrow], wide_in[token, columns], NN)

    for c in range(blocks):
        products(0, c, update, v, k)
    for copy in small[1:] + mat_copies:
        copy.wait()
    decay = decay_column(gammas, 0, heads, 1)
    factors = [kept_at(documents, seq * blocks + c) * decay for c in range(blocks)]
    state = update[0]
    for c in range(1, blocks):
        state = update[c] + factors[c] * dot_exact(state, mats[c], NT)
    carried = None
    for c in reversed(range(blocks)):
        products(1, c, source, dy, q)
        total = source[c] if carried is None else source[c] + carried
        carried = factors[c] * dot_exact(total, mats[c], NN)
    upper = lax.rem(seq, 2) == 1
    for i, value in enumerate((state, carried)):
        first, second = value[:half], value[half:]
        held[i] = jnp.where(upper, second, first)
        sent[i] = jnp.where(upper, first, second)


def near_step():
    return 1 + lax.rem(lax.axis_index("head"), 2)


def swap_near(x, first):
    devices, ways = lax.axis_size("seq"), lax.axis_size("head")
    pairs = []
    for seq in range(devices):
        for head in range(ways):
            by = 1 + head % 2 if first else 2 - head % 2
            pairs.append((seq * ways + head, (seq ^ by) * ways + head))
    return lax.ppermute(x, ("seq", "head"), pairs)


def maps_kernel(
    blocks, heads, reach, masks, regimes, documents, gammas, transitions,
    device_maps, powers, factors, weights, *rest,
):
    seq = lax.axis_index("seq")
    level = lax.div(seq, 2)
    last_block = documents.shape[0] - 1
    far, (mats, mat_sems) = rest[:-2], rest[-2:]
    first = (level - reach + 1) * 2 * blocks
    copies = []
    for i in range(mats.shape[0]):
        block = jnp.clip(first + i, 0, last_block)
        copies.append(
            pltpu.make_async_copy(transitions.at[regimes[block]], mats.at[i], mat_sems.at[i])
        )
        copies[-1].start()
    for i in range(reach):
        powers[i] = decay_column(gammas, 0, heads, blocks * max(1, 2 * i))
    decay = decay_column(gammas, 0, heads, 1)
    for c in range(blocks):
        factors[c] = kept_at(documents, seq * blocks + c) * decay
    near = near_step()
    owned = weights.shape[1]
    sources = [seq ^ mask for mask in masks]
    sources += [x ^ near for x in sources]
    for i, source in enumerate(sources):
        for c in range(blocks):
            regime = regimes[source * blocks + c]
            at = slice(i * blocks + c, i * blocks + c + 1)
            for j, owner in enumerate((seq ^ (3 - near), seq)):
                for r in range(owned):
                    match = jnp.where(regime == owner * owned + r, 1.0, 0.0).astype(F32)
                    weights[j, r, at, :] = jnp.full((1, STATE), match)

    for copy in copies:
        copy.wait()

    def device_map(device):
        result = None
        for c in range(blocks):
            block = jnp.clip(device * blocks + c, 0, last_block)
            mat = mats[device * blocks + c - first]
            kept = kept_at(documents, block)
            if result is None:
                result = mat.astype(F32)
            elif c == 1:
                result = dot(mat, result.astype(BF16), NN)
            else:
                high, low = halves(result)
                result = dot(mat, high, NN) + dot(mat, low, NN)
            result = result * kept
        return result

    def pair_map(at):
        low = halves(device_map(at * 2))
        high = halves(device_map(at * 2 + 1))
        return dot_pair(high, low, NN)

    for i in range(2):
        device_maps[i, 0], device_maps[i, 1] = halves(device_map(level * 2 + i))
    if reach > 1:
        far = far[0]
        forward = backward = None
        for distance in range(2, reach + 1):
            behind = pair_map(level - distance + 1)
            ahead = pair_map(level + distance - 1)
            if forward is None:
                forward, backward = behind, ahead
            else:
                forward = dot_pair(halves(forward), halves(behind), NN)
                backward = dot_pair(halves(ahead), halves(backward), NN)
            far[distance - 2, 0, 0], far[distance - 2, 0, 1] = halves(forward)
            far[distance - 2, 1, 0], far[distance - 2, 1, 1] = halves(backward)


def half_rows(columns, i, upper):
    half = columns.shape[1] // 2
    return columns[i, pl.ds(pl.multiple_of(upper * half, half), half), :]


def pair_kernel(routes, powers, held, arrived, device_maps, *outs):
    seq = lax.axis_index("seq")
    level, upper = lax.div(seq, 2), lax.rem(seq, 2)
    is_upper = upper == 1
    decay = half_rows(powers, 0, upper)
    ends = [jnp.where(is_upper, arrived[0], held[0]), jnp.where(is_upper, held[0], arrived[0])]
    starts = [jnp.where(is_upper, arrived[1], held[1]), jnp.where(is_upper, held[1], arrived[1])]
    low_map = (device_maps[0, 0], device_maps[0, 1])
    high_map = (device_maps[1, 0], device_maps[1, 1])
    forward = ends[1] + decay * dot_pair(halves(ends[0]), high_map, NT)
    backward = starts[0] + decay * dot_pair(halves(starts[1]), low_map, NN)
    for out, (distance, parity) in zip(outs, routes):
        ahead = lax.rem(lax.div(level, distance), 2) == parity
        out[...] = jnp.where(ahead, forward, backward)


def entry_kernel(reach, routes, powers, held, arrived, device_maps, *rest):
    count = len(routes)
    received, (own, sent) = rest[:count], rest[-2:]
    far = rest[count] if reach > 1 else None
    seq = lax.axis_index("seq")
    level, upper = lax.div(seq, 2), lax.rem(seq, 2)
    is_upper = upper == 1
    decay = half_rows(powers, 0, upper)
    found = dict(zip(routes, received))
    forward = backward = None
    for distance in range(1, reach + 1):
        even = found[distance, 0][...]
        odd = found[distance, 1][...] if (distance, 1) in found else jnp.zeros_like(even)
        flip = lax.rem(lax.div(level, distance), 2) == 1
        behind = jnp.where(flip, even, odd)
        ahead = jnp.where(flip, odd, even)
        if distance == 1:
            forward, backward = behind, ahead
        else:
            power = half_rows(powers, distance - 1, upper)
            i = distance - 2
            forward += power * dot_pair(halves(behind), (far[i, 0, 0], far[i, 0, 1]), NT)
            backward += power * dot_pair(halves(ahead), (far[i, 1, 0], far[i, 1, 1]), NN)
    low_map = (device_maps[0, 0], device_maps[0, 1])
    high_map = (device_maps[1, 0], device_maps[1, 1])
    low_end = jnp.where(is_upper, arrived[0], held[0])
    high_start = jnp.where(is_upper, held[1], arrived[1])
    inner_forward = low_end + decay * dot_pair(halves(forward), low_map, NT)
    inner_backward = high_start + decay * dot_pair(halves(backward), high_map, NN)
    own[0] = jnp.where(is_upper, inner_forward, forward)
    own[1] = jnp.where(is_upper, backward, inner_backward)
    sent[0] = jnp.where(is_upper, forward, inner_forward)
    sent[1] = jnp.where(is_upper, inner_backward, backward)


def states_of(blocks, factors, own, arrived, update, source, mats):
    upper = lax.rem(lax.axis_index("seq"), 2) == 1

    def whole(i):
        first = jnp.where(upper, arrived[i], own[i])
        second = jnp.where(upper, own[i], arrived[i])
        return jnp.concatenate([first, second], axis=0)

    before, carried = whole(0), whole(1)
    befores, entries, leaves, totals = [], [], [None] * blocks, [None] * blocks
    for c in range(blocks):
        befores.append(halves(before))
        high, low = befores[-1]
        entry = factors[c] * (dot(high, mats[c], NT) + dot(low, mats[c], NT))
        entries.append(entry)
        before = entry + update[c]
    for c in reversed(range(blocks)):
        leaves[c] = carried
        totals[c] = source[c] + carried
        if c > 0:
            carried = factors[c] * dot_exact(totals[c], mats[c], NN)
    return befores, entries, leaves, totals


def terms_kernel(blocks, ways, factors, own, arrived, update, source, mats, held, sent, term):
    head = lax.axis_index("head")
    befores, _, _, totals = states_of(blocks, factors, own, arrived, update, source, mats)
    part = STATE // ways
    core = lax.rem(head, 2)
    for c in range(blocks):
        term[...] = dot_pair(halves(factors[c] * totals[c]), befores[c], TN)
        for i in range(ways // 2):
            held[i, c] = term[pl.ds(pl.multiple_of((2 * i + core) * part, part), part), :]
            sent[i, c] = term[pl.ds(pl.multiple_of((2 * i + 1 - core) * part, part), part), :]


def rounded_kernel(blocks, factors, own, arrived, update, source, mats, entries, leaves):
    _, entry, leave, _ = states_of(blocks, factors, own, arrived, update, source, mats)
    for c in range(blocks):
        entries[c] = entry[c].astype(BF16)
        leaves[c] = leave[c].astype(BF16)


def regime_kernel(owner, weights, *rest):
    pieces, out = rest[:-1], rest[-1]
    blocks = pieces[0].shape[0]
    for r in range(out.shape[0]):
        total = None
        for i, piece in enumerate(pieces):
            for c in range(blocks):
                at = i * blocks + c
                value = weights[owner, r, at : at + 1, :] * piece[c]
                total = value if total is None else total + value
        out[r] = total


def add_kernel(a, b, out):
    out[...] = a[...] + b[...]


def within_kernel(q, k, v, dy, entries, leaves, *rest):
    dq, dk, dv = rest[-3:]
    row = lax.broadcasted_iota(jnp.int32, (BLOCK, BLOCK), 0)
    column = lax.broadcasted_iota(jnp.int32, (BLOCK, BLOCK), 1)
    lower, upper = row >= column, row <= column
    for h in range(v.shape[1] // HEAD_DIM):
        wide = slice(h * STATE, (h + 1) * STATE)
        narrow = slice(h * HEAD_DIM, (h + 1) * HEAD_DIM)
        qh, kh, vh, gh = q[:, wide], k[:, wide], v[:, narrow], dy[:, narrow]
        entry, leave = entries[0, narrow, :], leaves[0, narrow, :]
        probs_t = jnp.where(upper, dot(kh, qh, NT), 0.0).astype(BF16)
        dscore = jnp.where(lower, dot(gh, vh, NT), 0.0).astype(BF16)
        dscore_t = jnp.where(upper, dot(vh, gh, NT), 0.0).astype(BF16)
        dq[:, wide] = (dot(gh, entry, NN) + dot(dscore, kh, NN)).astype(BF16)
        dk[:, wide] = (dot(vh, leave, NN) + dot(dscore_t, qh, NN)).astype(BF16)
        dv[:, narrow] = (dot(kh, leave, NT) + dot(probs_t, gh, NN)).astype(BF16)


def swap(x, axis, by):
    count = lax.axis_size(axis)
    return lax.ppermute(x, axis, [(i, i ^ by) for i in range(count)])


def level_route(x, distance, parity):
    levels = lax.axis_size("seq") // 2
    pairs = []
    for low in range(levels - distance):
        if (low // distance) % 2 == parity:
            for side in range(2):
                a, b = 2 * low + side, 2 * (low + distance) + side
                pairs += [(a, b), (b, a)]
    return lax.ppermute(x, "seq", pairs)


def routes_up_to(reach, levels):
    return [
        (distance, parity)
        for distance in range(1, reach + 1)
        for parity in range(2)
        if any((low // distance) % 2 == parity for low in range(levels - distance))
    ]


def local(queries, keys, values, out_grad, transitions, gammas, regimes, documents):
    tokens_dev = queries.shape[0]
    heads = gammas.shape[0]
    blocks = tokens_dev // BLOCK
    all_blocks = documents.shape[0]
    devices, ways = lax.axis_size("seq"), lax.axis_size("head")
    levels = devices // 2
    rows = heads * HEAD_DIM
    half = rows // 2
    reach = min(levels - 1, -(-(all_blocks // 2 - 1) // (2 * blocks)))
    routes = routes_up_to(reach, levels)[::-1]
    head = lax.axis_index("head")
    owned, part = REGIMES // devices, STATE // ways
    steps = [devices - 2] + [1 << i for i in range(2, levels.bit_length() - 1)][::-1]
    masks = [0]
    for by in steps:
        masks += [x ^ by for x in masks]

    def shape(*dims, dtype=F32):
        return jax.ShapeDtypeStruct(dims, dtype)

    state_shape = shape(blocks, rows, STATE)
    half_shape = shape(2, half, STATE)
    outs = (state_shape, state_shape, half_shape, half_shape)
    def in_hbm(x):
        return pltpu.with_memory_space_constraint(x, pltpu.HBM)

    def in_vmem(x):
        return pltpu.VMEM(x.shape, x.dtype)

    mat_shape = shape(blocks, STATE, STATE, dtype=BF16)
    inputs = (queries, keys, values, out_grad)
    update, source, sent, held, mats = pl.pallas_call(
        functools.partial(local_kernel, blocks, heads),
        in_specs=[HBM] * 8,
        out_specs=(VMEM,) * 5,
        out_shape=tuple(in_vmem(x) for x in outs + (mat_shape,)),
        scratch_shapes=[in_vmem(x) for x in inputs]
        + [
            pltpu.SMEM(regimes.shape, jnp.int32),
            pltpu.SMEM(documents.shape, jnp.int32),
            pltpu.SMEM(gammas.shape, F32),
            pltpu.SemaphoreType.DMA((3,)),
            pltpu.SemaphoreType.DMA((blocks,)),
            pltpu.SemaphoreType.DMA((2,)),
            pltpu.SemaphoreType.DMA((2, blocks)),
        ],
        compiler_params=PARAMS,
    )(
        *[in_hbm(x) for x in (regimes, documents, gammas, transitions) + inputs]
    )

    arrived = swap(sent, "seq", 1)
    map_shapes = (
        shape(2, 2, STATE, STATE, dtype=BF16),
        shape(reach, rows, 1),
        shape(blocks, rows, 1),
        shape(2, owned, 2 * len(masks) * blocks, STATE),
    )
    if reach > 1:
        map_shapes += (shape(reach - 1, 2, 2, STATE, STATE, dtype=BF16),)
    needed = (2 * reach - 1) * 2 * blocks
    device_maps, powers, factors, weights, *far = pl.pallas_call(
        functools.partial(maps_kernel, blocks, heads, reach, masks),
        in_specs=[SMEM, SMEM, SMEM, HBM],
        out_specs=(VMEM,) * len(map_shapes),
        out_shape=map_shapes,
        scratch_shapes=[
            pltpu.VMEM((needed, STATE, STATE), BF16),
            pltpu.SemaphoreType.DMA((needed,)),
        ],
        compiler_params=PARAMS,
    )(regimes, documents, gammas, in_hbm(transitions))

    trades = pl.pallas_call(
        functools.partial(pair_kernel, routes),
        in_specs=[VMEM] * 4,
        out_specs=(VMEM,) * len(routes),
        out_shape=(shape(half, STATE),) * len(routes),
        compiler_params=PARAMS,
    )(powers, held, arrived, device_maps)
    received = [level_route(x, *route) for x, route in zip(trades, routes)]

    own, sent_entry = pl.pallas_call(
        functools.partial(entry_kernel, reach, routes),
        in_specs=[VMEM] * (4 + len(received) + len(far)),
        out_specs=(VMEM, VMEM),
        out_shape=(half_shape, half_shape),
        compiler_params=PARAMS,
    )(powers, held, arrived, device_maps, *received, *far)
    arrived_entry = swap(sent_entry, "seq", 1)

    part_shape = shape(ways // 2, blocks, part, STATE)
    bf16_states = shape(blocks, rows, STATE, dtype=BF16)
    states = (factors, own, arrived_entry, update, source, mats)

    def states_call(kernel, states, outs, scratch):
        return pl.pallas_call(
            kernel,
            in_specs=[VMEM] * len(states),
            out_specs=(VMEM,) * len(outs),
            out_shape=outs,
            scratch_shapes=scratch,
            compiler_params=PARAMS,
        )(*states)

    held_term, sent_term = states_call(
        functools.partial(terms_kernel, blocks, ways),
        states,
        (part_shape, part_shape),
        [pltpu.VMEM((STATE, STATE), F32)],
    )

    def output_call(c, entries, leaves, before):
        wide = pl.BlockSpec((BLOCK, 2 * STATE), lambda h: (c, h))
        narrow = pl.BlockSpec((BLOCK, 2 * HEAD_DIM), lambda h: (c, h))
        state = pl.BlockSpec((1, 2 * HEAD_DIM, STATE), lambda h: (c, h, 0))
        return pl.pallas_call(
            within_kernel,
            grid=(heads // 2,),
            in_specs=[wide, wide, narrow, narrow, state, state] + [HBM] * len(before),
            out_specs=[wide, wide, narrow],
            out_shape=[shape(*x.shape, dtype=BF16) for x in inputs[:3]],
            input_output_aliases={6 + i: i for i in range(len(before))},
            compiler_params=PARAMS,
            cost_estimate=pl.CostEstimate(
                flops=20 * heads * BLOCK * BLOCK * STATE,
                bytes_accessed=3 << 20,
                transcendentals=0,
            ),
        )(*[in_hbm(x) for x in inputs], entries, leaves, *before)

    sent_term, states = lax.optimization_barrier((sent_term, states))
    arrived_term = swap(sent_term, "head", 1)
    entries, leaves = states_call(
        functools.partial(rounded_kernel, blocks), states, (bf16_states, bf16_states), []
    )
    arrived_term, entries, leaves = lax.optimization_barrier((arrived_term, entries, leaves))
    summed = held_term + arrived_term
    by, grads = 2, ()
    while by < ways:
        split = summed.reshape(-1, 2, blocks, part, STATE)
        bit = lax.rem(lax.div(head, by), 2)
        going = lax.dynamic_index_in_dim(split, 1 - bit, 1, keepdims=False)
        staying = lax.dynamic_index_in_dim(split, bit, 1, keepdims=False)
        going, entries, leaves = lax.optimization_barrier((going, entries, leaves))
        arrived_part = swap(going, "head", by)
        if not grads:
            grads = output_call(0, entries, leaves, ())
            arrived_part, grads = lax.optimization_barrier((arrived_part, grads))
        summed = staying + arrived_part
        by *= 2
    summed = summed.reshape(blocks, part, STATE)

    pieces = [summed]
    for by in steps:
        pieces += [swap(x, "seq", by) for x in pieces]
    near = swap_near(summed, True)
    pieces += [near] + [swap_near(x, True) for x in pieces[1:]]

    def regime_sum(owner):
        return pl.pallas_call(
            functools.partial(regime_kernel, owner),
            in_specs=[VMEM] * (1 + len(pieces)),
            out_specs=VMEM,
            out_shape=shape(owned, part, STATE),
            compiler_params=PARAMS,
        )(weights, *pieces)

    sent_sum = regime_sum(0)
    sent_sum, grads = lax.optimization_barrier((sent_sum, grads))
    arrived_sum = swap_near(sent_sum, False)
    for c in range(1, blocks):
        grads = output_call(c, entries, leaves, grads)
    own_sum = regime_sum(1)
    arrived_sum, own_sum, grads = lax.optimization_barrier((arrived_sum, own_sum, grads))
    regime_grad = pl.pallas_call(
        add_kernel,
        in_specs=[VMEM, VMEM],
        out_specs=VMEM,
        out_shape=shape(owned, part, STATE),
        compiler_params=PARAMS,
    )(own_sum, arrived_sum)
    return (*grads, regime_grad)


def solution(mesh):
    in_specs = (
        P("seq", "head"),
        P("seq", "head"),
        P("seq", "head"),
        P("seq", "head"),
        P(),
        P("head"),
        P(),
        P(),
    )
    out_specs = (P("seq", "head"), P("seq", "head"), P("seq", "head"), P("seq", "head", None))
    return jax.shard_map(local, mesh=mesh, in_specs=in_specs, out_specs=out_specs, check_vma=False)
```

```python
import functools

import jax
import jax.numpy as jnp
from jax import lax
from jax.experimental import pallas as pl
from jax.experimental.pallas import tpu as pltpu
from jax.sharding import PartitionSpec as P

STATE = 256
HEAD_DIM = 64
REGIMES = 32
BLOCK = 256

F32 = jnp.float32
BF16 = jnp.bfloat16
NN = (((1,), (0,)), ((), ()))
NT = (((1,), (1,)), ((), ()))
TN = (((0,), (0,)), ((), ()))
VMEM = pl.BlockSpec(memory_space=pltpu.VMEM)
SMEM = pl.BlockSpec(memory_space=pltpu.SMEM)
HBM = pl.BlockSpec(memory_space=pltpu.HBM)
PARAMS = pltpu.CompilerParams(vmem_limit_bytes=32 << 20)


def dot(a, b, dims):
    return lax.dot_general(a, b, dims, preferred_element_type=F32)


def halves(x):
    high = x.astype(BF16)
    return high, (x - high.astype(F32)).astype(BF16)


def dot_exact(x, matrix, dims):
    high, low = halves(x)
    return dot(high, matrix, dims) + dot(low, matrix, dims)


def dot_pair(a, b, dims):
    return dot(a[0], b[0], dims) + (dot(a[0], b[1], dims) + dot(a[1], b[0], dims))


def kept_at(documents, block):
    before = documents[jnp.maximum(block - 1, 0)]
    same = jnp.where(documents[block] == before, 1.0, 0.0)
    return jnp.where(block > 0, same, 0.0).astype(F32)


def decay_column(gammas, first, count, power):
    parts = []
    for i in range(count):
        g = gammas[first + i]
        value = g
        for _ in range(power - 1):
            value = value * g
        parts.append(jnp.full((HEAD_DIM, 1), value, F32))
    return jnp.concatenate(parts, axis=0)


def local_kernel(
    blocks, heads, regimes_hbm, documents_hbm, gammas_hbm, transitions, q_hbm, k_hbm, v_hbm, dy_hbm,
    update, source, sent, held, mats,
    q, k, v, dy, regimes, documents, gammas, small_sems, mat_sems, row_sems, wide_sems,
):
    seq = lax.axis_index("seq")
    half = heads * HEAD_DIM // 2
    small = [
        pltpu.make_async_copy(a, b, small_sems.at[i])
        for i, (a, b) in enumerate(
            ((regimes_hbm, regimes), (documents_hbm, documents), (gammas_hbm, gammas))
        )
    ]
    for copy in small:
        copy.start()
    rows, wide = [], {}
    for i, (a, b) in enumerate(((v_hbm, v), (dy_hbm, dy))):
        rows.append(pltpu.make_async_copy(a, b, row_sems.at[i]))
    rows[0].start()
    for i, (a, b) in enumerate(((k_hbm, k), (q_hbm, q))):
        wide[i] = pltpu.make_async_copy(a, b, wide_sems.at[i, 0])
        wide[i].start()
        if i == 0:
            rows[1].start()
    small[0].wait()
    mat_copies = []
    for c in range(blocks):
        copy = pltpu.make_async_copy(
            transitions.at[regimes[seq * blocks + c]], mats.at[c], mat_sems.at[c]
        )
        copy.start()
        mat_copies.append(copy)
    def products(i, c, out, narrow_in, wide_in):
        token = slice(c * BLOCK, (c + 1) * BLOCK)
        if c == (0, blocks - 1)[i]:
            rows[i].wait()
        flipped = narrow_in[token, :].T
        if c == (0, blocks - 1)[i]:
            wide[i].wait()
        for h in range(heads):
            columns = slice(h * STATE, (h + 1) * STATE)
            narrow = slice(h * HEAD_DIM, (h + 1) * HEAD_DIM)
            out[c, narrow, :] = dot(flipped[narrow], wide_in[token, columns], NN)

    for c in range(blocks):
        products(0, c, update, v, k)
    for copy in small[1:] + mat_copies:
        copy.wait()
    decay = decay_column(gammas, 0, heads, 1)
    factors = [kept_at(documents, seq * blocks + c) * decay for c in range(blocks)]
    state = update[0]
    for c in range(1, blocks):
        state = update[c] + factors[c] * dot_exact(state, mats[c], NT)
    carried = None
    for c in reversed(range(blocks)):
        products(1, c, source, dy, q)
        total = source[c] if carried is None else source[c] + carried
        carried = factors[c] * dot_exact(total, mats[c], NN)
    upper = lax.rem(seq, 2) == 1
    for i, value in enumerate((state, carried)):
        first, second = value[:half], value[half:]
        held[i] = jnp.where(upper, second, first)
        sent[i] = jnp.where(upper, first, second)


def near_step():
    return 1 + lax.rem(lax.axis_index("head"), 2)


def swap_near(x, first):
    devices, ways = lax.axis_size("seq"), lax.axis_size("head")
    pairs = []
    for seq in range(devices):
        for head in range(ways):
            by = 1 + head % 2 if first else 2 - head % 2
            pairs.append((seq * ways + head, (seq ^ by) * ways + head))
    return lax.ppermute(x, ("seq", "head"), pairs)


def maps_kernel(
    blocks, heads, reach, masks, regimes, documents, gammas, transitions,
    device_maps, powers, factors, weights, *rest,
):
    seq = lax.axis_index("seq")
    level = lax.div(seq, 2)
    last_block = documents.shape[0] - 1
    far, (mats, mat_sems) = rest[:-2], rest[-2:]
    first = (level - reach + 1) * 2 * blocks
    copies = []
    for i in range(mats.shape[0]):
        block = jnp.clip(first + i, 0, last_block)
        copies.append(
            pltpu.make_async_copy(transitions.at[regimes[block]], mats.at[i], mat_sems.at[i])
        )
        copies[-1].start()
    for i in range(reach):
        powers[i] = decay_column(gammas, 0, heads, blocks * max(1, 2 * i))
    decay = decay_column(gammas, 0, heads, 1)
    for c in range(blocks):
        factors[c] = kept_at(documents, seq * blocks + c) * decay
    near = near_step()
    owned = weights.shape[1]
    sources = [seq ^ mask for mask in masks]
    sources += [x ^ near for x in sources]
    for i, source in enumerate(sources):
        for c in range(blocks):
            regime = regimes[source * blocks + c]
            at = slice(i * blocks + c, i * blocks + c + 1)
            for j, owner in enumerate((seq ^ (3 - near), seq)):
                for r in range(owned):
                    match = jnp.where(regime == owner * owned + r, 1.0, 0.0).astype(F32)
                    weights[j, r, at, :] = jnp.full((1, STATE), match)

    for copy in copies:
        copy.wait()

    def device_map(device):
        result = None
        for c in range(blocks):
            block = jnp.clip(device * blocks + c, 0, last_block)
            mat = mats[device * blocks + c - first]
            kept = kept_at(documents, block)
            if result is None:
                result = mat.astype(F32)
            elif c == 1:
                result = dot(mat, result.astype(BF16), NN)
            else:
                high, low = halves(result)
                result = dot(mat, high, NN) + dot(mat, low, NN)
            result = result * kept
        return result

    def pair_map(at):
        low = halves(device_map(at * 2))
        high = halves(device_map(at * 2 + 1))
        return dot_pair(high, low, NN)

    for i in range(2):
        device_maps[i, 0], device_maps[i, 1] = halves(device_map(level * 2 + i))
    if reach > 1:
        far = far[0]
        forward = backward = None
        for distance in range(2, reach + 1):
            behind = pair_map(level - distance + 1)
            ahead = pair_map(level + distance - 1)
            if forward is None:
                forward, backward = behind, ahead
            else:
                forward = dot_pair(halves(forward), halves(behind), NN)
                backward = dot_pair(halves(ahead), halves(backward), NN)
            far[distance - 2, 0, 0], far[distance - 2, 0, 1] = halves(forward)
            far[distance - 2, 1, 0], far[distance - 2, 1, 1] = halves(backward)


def half_rows(columns, i, upper):
    half = columns.shape[1] // 2
    return columns[i, pl.ds(pl.multiple_of(upper * half, half), half), :]


def pair_kernel(routes, powers, held, arrived, device_maps, *outs):
    seq = lax.axis_index("seq")
    level, upper = lax.div(seq, 2), lax.rem(seq, 2)
    is_upper = upper == 1
    decay = half_rows(powers, 0, upper)
    ends = [jnp.where(is_upper, arrived[0], held[0]), jnp.where(is_upper, held[0], arrived[0])]
    starts = [jnp.where(is_upper, arrived[1], held[1]), jnp.where(is_upper, held[1], arrived[1])]
    low_map = (device_maps[0, 0], device_maps[0, 1])
    high_map = (device_maps[1, 0], device_maps[1, 1])
    forward = ends[1] + decay * dot_pair(halves(ends[0]), high_map, NT)
    backward = starts[0] + decay * dot_pair(halves(starts[1]), low_map, NN)
    for out, (distance, parity) in zip(outs, routes):
        ahead = lax.rem(lax.div(level, distance), 2) == parity
        out[...] = jnp.where(ahead, forward, backward)


def entry_kernel(reach, routes, powers, held, arrived, device_maps, *rest):
    count = len(routes)
    received, (own, sent) = rest[:count], rest[-2:]
    far = rest[count] if reach > 1 else None
    seq = lax.axis_index("seq")
    level, upper = lax.div(seq, 2), lax.rem(seq, 2)
    is_upper = upper == 1
    decay = half_rows(powers, 0, upper)
    found = dict(zip(routes, received))
    forward = backward = None
    for distance in range(1, reach + 1):
        even = found[distance, 0][...]
        odd = found[distance, 1][...] if (distance, 1) in found else jnp.zeros_like(even)
        flip = lax.rem(lax.div(level, distance), 2) == 1
        behind = jnp.where(flip, even, odd)
        ahead = jnp.where(flip, odd, even)
        if distance == 1:
            forward, backward = behind, ahead
        else:
            power = half_rows(powers, distance - 1, upper)
            i = distance - 2
            forward += power * dot_pair(halves(behind), (far[i, 0, 0], far[i, 0, 1]), NT)
            backward += power * dot_pair(halves(ahead), (far[i, 1, 0], far[i, 1, 1]), NN)
    low_map = (device_maps[0, 0], device_maps[0, 1])
    high_map = (device_maps[1, 0], device_maps[1, 1])
    low_end = jnp.where(is_upper, arrived[0], held[0])
    high_start = jnp.where(is_upper, held[1], arrived[1])
    inner_forward = low_end + decay * dot_pair(halves(forward), low_map, NT)
    inner_backward = high_start + decay * dot_pair(halves(backward), high_map, NN)
    own[0] = jnp.where(is_upper, inner_forward, forward)
    own[1] = jnp.where(is_upper, backward, inner_backward)
    sent[0] = jnp.where(is_upper, forward, inner_forward)
    sent[1] = jnp.where(is_upper, inner_backward, backward)


def states_of(blocks, factors, own, arrived, update, source, mats):
    upper = lax.rem(lax.axis_index("seq"), 2) == 1

    def whole(i):
        first = jnp.where(upper, arrived[i], own[i])
        second = jnp.where(upper, own[i], arrived[i])
        return jnp.concatenate([first, second], axis=0)

    before, carried = whole(0), whole(1)
    befores, entries, leaves, totals = [], [], [None] * blocks, [None] * blocks
    for c in range(blocks):
        befores.append(halves(before))
        high, low = befores[-1]
        entry = factors[c] * (dot(high, mats[c], NT) + dot(low, mats[c], NT))
        entries.append(entry)
        before = entry + update[c]
    for c in reversed(range(blocks)):
        leaves[c] = carried
        totals[c] = source[c] + carried
        if c > 0:
            carried = factors[c] * dot_exact(totals[c], mats[c], NN)
    return befores, entries, leaves, totals


def half_terms(blocks, side, factors, entering, update, source, mats):
    half = entering.shape[1]
    rows = pl.ds(pl.multiple_of(side * half, half), half)
    before, carried = entering[0], entering[1]
    befores, totals = [], [None] * blocks
    for c in range(blocks):
        befores.append(halves(before))
        if c + 1 < blocks:
            high, low = befores[c]
            entry = dot(high, mats[c], NT) + dot(low, mats[c], NT)
            before = factors[c, rows, :] * entry + update[c, rows, :]
    for c in reversed(range(blocks)):
        totals[c] = source[c, rows, :] + carried
        if c > 0:
            carried = factors[c, rows, :] * dot_exact(totals[c], mats[c], NN)
    return [
        dot_pair(halves(factors[c, rows, :] * totals[c]), befores[c], TN) for c in range(blocks)
    ]


def own_terms_kernel(blocks, factors, own, update, source, mats, out):
    side = lax.rem(lax.axis_index("seq"), 2)
    for c, term in enumerate(half_terms(blocks, side, factors, own, update, source, mats)):
        out[c] = term


def terms_kernel(
    blocks, ways, factors, own_terms, arrived, update, source, mats, held, sent, term
):
    head = lax.axis_index("head")
    side = 1 - lax.rem(lax.axis_index("seq"), 2)
    part = STATE // ways
    core = lax.rem(head, 2)
    terms = half_terms(blocks, side, factors, arrived, update, source, mats)
    for c in range(blocks):
        term[...] = own_terms[c] + terms[c]
        for i in range(ways // 2):
            held[i, c] = term[pl.ds(pl.multiple_of((2 * i + core) * part, part), part), :]
            sent[i, c] = term[pl.ds(pl.multiple_of((2 * i + 1 - core) * part, part), part), :]


def rounded_kernel(blocks, factors, own, arrived, update, source, mats, entries, leaves):
    _, entry, leave, _ = states_of(blocks, factors, own, arrived, update, source, mats)
    for c in range(blocks):
        entries[c] = entry[c].astype(BF16)
        leaves[c] = leave[c].astype(BF16)


def regime_kernel(owner, weights, *rest):
    pieces, out = rest[:-1], rest[-1]
    blocks = pieces[0].shape[0]
    for r in range(out.shape[0]):
        total = None
        for i, piece in enumerate(pieces):
            for c in range(blocks):
                at = i * blocks + c
                value = weights[owner, r, at : at + 1, :] * piece[c]
                total = value if total is None else total + value
        out[r] = total


def add_kernel(a, b, out):
    out[...] = a[...] + b[...]


def within_kernel(q, k, v, dy, entries, leaves, *rest):
    dq, dk, dv = rest[-3:]
    row = lax.broadcasted_iota(jnp.int32, (BLOCK, BLOCK), 0)
    column = lax.broadcasted_iota(jnp.int32, (BLOCK, BLOCK), 1)
    lower, upper = row >= column, row <= column
    for h in range(v.shape[1] // HEAD_DIM):
        wide = slice(h * STATE, (h + 1) * STATE)
        narrow = slice(h * HEAD_DIM, (h + 1) * HEAD_DIM)
        qh, kh, vh, gh = q[:, wide], k[:, wide], v[:, narrow], dy[:, narrow]
        entry, leave = entries[0, narrow, :], leaves[0, narrow, :]
        probs_t = jnp.where(upper, dot(kh, qh, NT), 0.0).astype(BF16)
        dscore = jnp.where(lower, dot(gh, vh, NT), 0.0).astype(BF16)
        dscore_t = jnp.where(upper, dot(vh, gh, NT), 0.0).astype(BF16)
        dq[:, wide] = (dot(gh, entry, NN) + dot(dscore, kh, NN)).astype(BF16)
        dk[:, wide] = (dot(vh, leave, NN) + dot(dscore_t, qh, NN)).astype(BF16)
        dv[:, narrow] = (dot(kh, leave, NT) + dot(probs_t, gh, NN)).astype(BF16)


def swap(x, axis, by):
    count = lax.axis_size(axis)
    return lax.ppermute(x, axis, [(i, i ^ by) for i in range(count)])


def level_route(x, distance, parity):
    levels = lax.axis_size("seq") // 2
    pairs = []
    for low in range(levels - distance):
        if (low // distance) % 2 == parity:
            for side in range(2):
                a, b = 2 * low + side, 2 * (low + distance) + side
                pairs += [(a, b), (b, a)]
    return lax.ppermute(x, "seq", pairs)


def routes_up_to(reach, levels):
    return [
        (distance, parity)
        for distance in range(1, reach + 1)
        for parity in range(2)
        if any((low // distance) % 2 == parity for low in range(levels - distance))
    ]


def local(queries, keys, values, out_grad, transitions, gammas, regimes, documents):
    tokens_dev = queries.shape[0]
    heads = gammas.shape[0]
    blocks = tokens_dev // BLOCK
    all_blocks = documents.shape[0]
    devices, ways = lax.axis_size("seq"), lax.axis_size("head")
    levels = devices // 2
    rows = heads * HEAD_DIM
    half = rows // 2
    reach = min(levels - 1, -(-(all_blocks // 2 - 1) // (2 * blocks)))
    routes = routes_up_to(reach, levels)[::-1]
    head = lax.axis_index("head")
    owned, part = REGIMES // devices, STATE // ways
    steps = [devices - 2] + [1 << i for i in range(2, levels.bit_length() - 1)][::-1]
    masks = [0]
    for by in steps:
        masks += [x ^ by for x in masks]

    def shape(*dims, dtype=F32):
        return jax.ShapeDtypeStruct(dims, dtype)

    state_shape = shape(blocks, rows, STATE)
    half_shape = shape(2, half, STATE)
    outs = (state_shape, state_shape, half_shape, half_shape)
    def in_hbm(x):
        return pltpu.with_memory_space_constraint(x, pltpu.HBM)

    def in_vmem(x):
        return pltpu.VMEM(x.shape, x.dtype)

    mat_shape = shape(blocks, STATE, STATE, dtype=BF16)
    inputs = (queries, keys, values, out_grad)
    update, source, sent, held, mats = pl.pallas_call(
        functools.partial(local_kernel, blocks, heads),
        in_specs=[HBM] * 8,
        out_specs=(VMEM,) * 5,
        out_shape=tuple(in_vmem(x) for x in outs + (mat_shape,)),
        scratch_shapes=[in_vmem(x) for x in inputs]
        + [
            pltpu.SMEM(regimes.shape, jnp.int32),
            pltpu.SMEM(documents.shape, jnp.int32),
            pltpu.SMEM(gammas.shape, F32),
            pltpu.SemaphoreType.DMA((3,)),
            pltpu.SemaphoreType.DMA((blocks,)),
            pltpu.SemaphoreType.DMA((2,)),
            pltpu.SemaphoreType.DMA((2, blocks)),
        ],
        compiler_params=PARAMS,
    )(
        *[in_hbm(x) for x in (regimes, documents, gammas, transitions) + inputs]
    )

    arrived = swap(sent, "seq", 1)
    map_shapes = (
        shape(2, 2, STATE, STATE, dtype=BF16),
        shape(reach, rows, 1),
        shape(blocks, rows, 1),
        shape(2, owned, 2 * len(masks) * blocks, STATE),
    )
    if reach > 1:
        map_shapes += (shape(reach - 1, 2, 2, STATE, STATE, dtype=BF16),)
    needed = (2 * reach - 1) * 2 * blocks
    device_maps, powers, factors, weights, *far = pl.pallas_call(
        functools.partial(maps_kernel, blocks, heads, reach, masks),
        in_specs=[SMEM, SMEM, SMEM, HBM],
        out_specs=(VMEM,) * len(map_shapes),
        out_shape=map_shapes,
        scratch_shapes=[
            pltpu.VMEM((needed, STATE, STATE), BF16),
            pltpu.SemaphoreType.DMA((needed,)),
        ],
        compiler_params=PARAMS,
    )(regimes, documents, gammas, in_hbm(transitions))

    trades = pl.pallas_call(
        functools.partial(pair_kernel, routes),
        in_specs=[VMEM] * 4,
        out_specs=(VMEM,) * len(routes),
        out_shape=(shape(half, STATE),) * len(routes),
        compiler_params=PARAMS,
    )(powers, held, arrived, device_maps)
    received = [level_route(x, *route) for x, route in zip(trades, routes)]

    own, sent_entry = pl.pallas_call(
        functools.partial(entry_kernel, reach, routes),
        in_specs=[VMEM] * (4 + len(received) + len(far)),
        out_specs=(VMEM, VMEM),
        out_shape=(half_shape, half_shape),
        compiler_params=PARAMS,
    )(powers, held, arrived, device_maps, *received, *far)
    arrived_entry = swap(sent_entry, "seq", 1)

    part_shape = shape(ways // 2, blocks, part, STATE)
    bf16_states = shape(blocks, rows, STATE, dtype=BF16)
    states = (factors, own, arrived_entry, update, source, mats)

    def states_call(kernel, states, outs, scratch):
        return pl.pallas_call(
            kernel,
            in_specs=[VMEM] * len(states),
            out_specs=(VMEM,) * len(outs),
            out_shape=outs,
            scratch_shapes=scratch,
            compiler_params=PARAMS,
        )(*states)

    (own_terms,) = states_call(
        functools.partial(own_terms_kernel, blocks),
        (factors, own, update, source, mats),
        (shape(blocks, STATE, STATE),),
        [],
    )
    held_term, sent_term = states_call(
        functools.partial(terms_kernel, blocks, ways),
        (factors, own_terms, arrived_entry, update, source, mats),
        (part_shape, part_shape),
        [pltpu.VMEM((STATE, STATE), F32)],
    )

    def output_call(c, entries, leaves, before):
        wide = pl.BlockSpec((BLOCK, 2 * STATE), lambda h: (c, h))
        narrow = pl.BlockSpec((BLOCK, 2 * HEAD_DIM), lambda h: (c, h))
        state = pl.BlockSpec((1, 2 * HEAD_DIM, STATE), lambda h: (c, h, 0))
        return pl.pallas_call(
            within_kernel,
            grid=(heads // 2,),
            in_specs=[wide, wide, narrow, narrow, state, state] + [HBM] * len(before),
            out_specs=[wide, wide, narrow],
            out_shape=[shape(*x.shape, dtype=BF16) for x in inputs[:3]],
            input_output_aliases={6 + i: i for i in range(len(before))},
            compiler_params=PARAMS,
            cost_estimate=pl.CostEstimate(
                flops=20 * heads * BLOCK * BLOCK * STATE,
                bytes_accessed=3 << 20,
                transcendentals=0,
            ),
        )(*[in_hbm(x) for x in inputs], entries, leaves, *before)

    sent_term, states = lax.optimization_barrier((sent_term, states))
    arrived_term = swap(sent_term, "head", 1)
    entries, leaves = states_call(
        functools.partial(rounded_kernel, blocks), states, (bf16_states, bf16_states), []
    )
    arrived_term, entries, leaves = lax.optimization_barrier((arrived_term, entries, leaves))
    summed = held_term + arrived_term
    by, grads = 2, ()
    while by < ways:
        split = summed.reshape(-1, 2, blocks, part, STATE)
        bit = lax.rem(lax.div(head, by), 2)
        going = lax.dynamic_index_in_dim(split, 1 - bit, 1, keepdims=False)
        staying = lax.dynamic_index_in_dim(split, bit, 1, keepdims=False)
        going, entries, leaves = lax.optimization_barrier((going, entries, leaves))
        arrived_part = swap(going, "head", by)
        if not grads:
            grads = output_call(0, entries, leaves, ())
            arrived_part, grads = lax.optimization_barrier((arrived_part, grads))
        summed = staying + arrived_part
        by *= 2
    summed = summed.reshape(blocks, part, STATE)

    pieces = [summed]
    for by in steps:
        pieces += [swap(x, "seq", by) for x in pieces]
    near = swap_near(summed, True)
    pieces += [near] + [swap_near(x, True) for x in pieces[1:]]

    def regime_sum(owner):
        return pl.pallas_call(
            functools.partial(regime_kernel, owner),
            in_specs=[VMEM] * (1 + len(pieces)),
            out_specs=VMEM,
            out_shape=shape(owned, part, STATE),
            compiler_params=PARAMS,
        )(weights, *pieces)

    sent_sum = regime_sum(0)
    sent_sum, grads = lax.optimization_barrier((sent_sum, grads))
    arrived_sum = swap_near(sent_sum, False)
    for c in range(1, blocks):
        grads = output_call(c, entries, leaves, grads)
    own_sum = regime_sum(1)
    arrived_sum, own_sum, grads = lax.optimization_barrier((arrived_sum, own_sum, grads))
    regime_grad = pl.pallas_call(
        add_kernel,
        in_specs=[VMEM, VMEM],
        out_specs=VMEM,
        out_shape=shape(owned, part, STATE),
        compiler_params=PARAMS,
    )(own_sum, arrived_sum)
    return (*grads, regime_grad)


def solution(mesh):
    in_specs = (
        P("seq", "head"),
        P("seq", "head"),
        P("seq", "head"),
        P("seq", "head"),
        P(),
        P("head"),
        P(),
        P(),
    )
    out_specs = (P("seq", "head"), P("seq", "head"), P("seq", "head"), P("seq", "head", None))
    return jax.shard_map(local, mesh=mesh, in_specs=in_specs, out_specs=out_specs, check_vma=False)
```

```python
import functools

import jax
import jax.numpy as jnp
from jax import lax
from jax.experimental import pallas as pl
from jax.experimental.pallas import tpu as pltpu
from jax.sharding import PartitionSpec as P

STATE = 256
HEAD_DIM = 64
REGIMES = 32
BLOCK = 256

F32 = jnp.float32
BF16 = jnp.bfloat16
NN = (((1,), (0,)), ((), ()))
NT = (((1,), (1,)), ((), ()))
TN = (((0,), (0,)), ((), ()))
VMEM = pl.BlockSpec(memory_space=pltpu.VMEM)
SMEM = pl.BlockSpec(memory_space=pltpu.SMEM)
HBM = pl.BlockSpec(memory_space=pltpu.HBM)
PARAMS = pltpu.CompilerParams(vmem_limit_bytes=32 << 20)


def dot(a, b, dims):
    return lax.dot_general(a, b, dims, preferred_element_type=F32)


def halves(x):
    high = x.astype(BF16)
    return high, (x - high.astype(F32)).astype(BF16)


def dot_exact(x, matrix, dims):
    high, low = halves(x)
    return dot(high, matrix, dims) + dot(low, matrix, dims)


def dot_pair(a, b, dims):
    return dot(a[0], b[0], dims) + (dot(a[0], b[1], dims) + dot(a[1], b[0], dims))


def kept_at(documents, block):
    before = documents[jnp.maximum(block - 1, 0)]
    same = jnp.where(documents[block] == before, 1.0, 0.0)
    return jnp.where(block > 0, same, 0.0).astype(F32)


def decay_column(gammas, first, count, power):
    parts = []
    for i in range(count):
        g = gammas[first + i]
        value = g
        for _ in range(power - 1):
            value = value * g
        parts.append(jnp.full((HEAD_DIM, 1), value, F32))
    return jnp.concatenate(parts, axis=0)


def local_kernel(
    blocks, heads, regimes_hbm, documents_hbm, gammas_hbm, transitions, q_hbm, k_hbm, v_hbm, dy_hbm,
    update, source, sent, held, mats,
    q, k, v, dy, regimes, documents, gammas, small_sems, mat_sems, row_sems, wide_sems,
):
    seq = lax.axis_index("seq")
    half = heads * HEAD_DIM // 2
    small = [
        pltpu.make_async_copy(a, b, small_sems.at[i])
        for i, (a, b) in enumerate(
            ((regimes_hbm, regimes), (documents_hbm, documents), (gammas_hbm, gammas))
        )
    ]
    for copy in small:
        copy.start()
    rows, wide = [], {}
    for i, (a, b) in enumerate(((v_hbm, v), (dy_hbm, dy))):
        rows.append(pltpu.make_async_copy(a, b, row_sems.at[i]))
    rows[0].start()
    for i, (a, b) in enumerate(((k_hbm, k), (q_hbm, q))):
        wide[i] = pltpu.make_async_copy(a, b, wide_sems.at[i, 0])
        wide[i].start()
        if i == 0:
            rows[1].start()
    small[0].wait()
    mat_copies = []
    for c in range(blocks):
        copy = pltpu.make_async_copy(
            transitions.at[regimes[seq * blocks + c]], mats.at[c], mat_sems.at[c]
        )
        copy.start()
        mat_copies.append(copy)
    def products(i, c, out, narrow_in, wide_in):
        token = slice(c * BLOCK, (c + 1) * BLOCK)
        if c == (0, blocks - 1)[i]:
            rows[i].wait()
        flipped = narrow_in[token, :].T
        if c == (0, blocks - 1)[i]:
            wide[i].wait()
        for h in range(heads):
            columns = slice(h * STATE, (h + 1) * STATE)
            narrow = slice(h * HEAD_DIM, (h + 1) * HEAD_DIM)
            out[c, narrow, :] = dot(flipped[narrow], wide_in[token, columns], NN)

    for c in range(blocks):
        products(0, c, update, v, k)
    for copy in small[1:] + mat_copies:
        copy.wait()
    decay = decay_column(gammas, 0, heads, 1)
    factors = [kept_at(documents, seq * blocks + c) * decay for c in range(blocks)]
    state = update[0]
    for c in range(1, blocks):
        state = update[c] + factors[c] * dot_exact(state, mats[c], NT)
    carried = None
    for c in reversed(range(blocks)):
        products(1, c, source, dy, q)
        total = source[c] if carried is None else source[c] + carried
        carried = factors[c] * dot_exact(total, mats[c], NN)
    upper = lax.rem(seq, 2) == 1
    for i, value in enumerate((state, carried)):
        first, second = value[:half], value[half:]
        held[i] = jnp.where(upper, second, first)
        sent[i] = jnp.where(upper, first, second)


def near_step():
    return 1 + lax.rem(lax.axis_index("head"), 2)


def swap_near(x, first):
    devices, ways = lax.axis_size("seq"), lax.axis_size("head")
    pairs = []
    for seq in range(devices):
        for head in range(ways):
            by = 1 + head % 2 if first else 2 - head % 2
            pairs.append((seq * ways + head, (seq ^ by) * ways + head))
    return lax.ppermute(x, ("seq", "head"), pairs)


def maps_kernel(
    blocks, heads, reach, masks, regimes, documents, gammas, transitions,
    device_maps, powers, factors, weights, *rest,
):
    seq = lax.axis_index("seq")
    level = lax.div(seq, 2)
    last_block = documents.shape[0] - 1
    far, (mats, mat_sems) = rest[:-2], rest[-2:]
    first = (level - reach + 1) * 2 * blocks
    copies = []
    for i in range(mats.shape[0]):
        block = jnp.clip(first + i, 0, last_block)
        copies.append(
            pltpu.make_async_copy(transitions.at[regimes[block]], mats.at[i], mat_sems.at[i])
        )
        copies[-1].start()
    for i in range(reach):
        powers[i] = decay_column(gammas, 0, heads, blocks * max(1, 2 * i))
    decay = decay_column(gammas, 0, heads, 1)
    for c in range(blocks):
        factors[c] = kept_at(documents, seq * blocks + c) * decay
    near = near_step()
    owned = weights.shape[1]
    sources = [seq ^ mask for mask in masks]
    sources += [x ^ near for x in sources]
    for i, source in enumerate(sources):
        for c in range(blocks):
            regime = regimes[source * blocks + c]
            at = slice(i * blocks + c, i * blocks + c + 1)
            for j, owner in enumerate((seq ^ (3 - near), seq)):
                for r in range(owned):
                    match = jnp.where(regime == owner * owned + r, 1.0, 0.0).astype(F32)
                    weights[j, r, at, :] = jnp.full((1, STATE), match)

    for copy in copies:
        copy.wait()

    def device_map(device):
        result = None
        for c in range(blocks):
            block = jnp.clip(device * blocks + c, 0, last_block)
            mat = mats[device * blocks + c - first]
            kept = kept_at(documents, block)
            if result is None:
                result = mat.astype(F32)
            elif c == 1:
                result = dot(mat, result.astype(BF16), NN)
            else:
                high, low = halves(result)
                result = dot(mat, high, NN) + dot(mat, low, NN)
            result = result * kept
        return result

    def pair_map(at):
        low = halves(device_map(at * 2))
        high = halves(device_map(at * 2 + 1))
        return dot_pair(high, low, NN)

    for i in range(2):
        device_maps[i, 0], device_maps[i, 1] = halves(device_map(level * 2 + i))
    if reach > 1:
        far = far[0]
        forward = backward = None
        for distance in range(2, reach + 1):
            behind = pair_map(level - distance + 1)
            ahead = pair_map(level + distance - 1)
            if forward is None:
                forward, backward = behind, ahead
            else:
                forward = dot_pair(halves(forward), halves(behind), NN)
                backward = dot_pair(halves(ahead), halves(backward), NN)
            far[distance - 2, 0, 0], far[distance - 2, 0, 1] = halves(forward)
            far[distance - 2, 1, 0], far[distance - 2, 1, 1] = halves(backward)


def half_rows(columns, i, upper):
    half = columns.shape[1] // 2
    return columns[i, pl.ds(pl.multiple_of(upper * half, half), half), :]


def pair_kernel(routes, powers, held, arrived, device_maps, *outs):
    seq = lax.axis_index("seq")
    level, upper = lax.div(seq, 2), lax.rem(seq, 2)
    is_upper = upper == 1
    decay = half_rows(powers, 0, upper)
    ends = [jnp.where(is_upper, arrived[0], held[0]), jnp.where(is_upper, held[0], arrived[0])]
    starts = [jnp.where(is_upper, arrived[1], held[1]), jnp.where(is_upper, held[1], arrived[1])]
    low_map = (device_maps[0, 0], device_maps[0, 1])
    high_map = (device_maps[1, 0], device_maps[1, 1])
    forward = ends[1] + decay * dot_pair(halves(ends[0]), high_map, NT)
    backward = starts[0] + decay * dot_pair(halves(starts[1]), low_map, NN)
    for out, (distance, parity) in zip(outs, routes):
        ahead = lax.rem(lax.div(level, distance), 2) == parity
        out[...] = jnp.where(ahead, forward, backward)


def entry_kernel(reach, routes, powers, held, arrived, device_maps, *rest):
    count = len(routes)
    received, (own, sent) = rest[:count], rest[-2:]
    far = rest[count] if reach > 1 else None
    seq = lax.axis_index("seq")
    level, upper = lax.div(seq, 2), lax.rem(seq, 2)
    is_upper = upper == 1
    decay = half_rows(powers, 0, upper)
    found = dict(zip(routes, received))
    forward = backward = None
    for distance in range(1, reach + 1):
        even = found[distance, 0][...]
        odd = found[distance, 1][...] if (distance, 1) in found else jnp.zeros_like(even)
        flip = lax.rem(lax.div(level, distance), 2) == 1
        behind = jnp.where(flip, even, odd)
        ahead = jnp.where(flip, odd, even)
        if distance == 1:
            forward, backward = behind, ahead
        else:
            power = half_rows(powers, distance - 1, upper)
            i = distance - 2
            forward += power * dot_pair(halves(behind), (far[i, 0, 0], far[i, 0, 1]), NT)
            backward += power * dot_pair(halves(ahead), (far[i, 1, 0], far[i, 1, 1]), NN)
    low_map = (device_maps[0, 0], device_maps[0, 1])
    high_map = (device_maps[1, 0], device_maps[1, 1])
    low_end = jnp.where(is_upper, arrived[0], held[0])
    high_start = jnp.where(is_upper, held[1], arrived[1])
    inner_forward = low_end + decay * dot_pair(halves(forward), low_map, NT)
    inner_backward = high_start + decay * dot_pair(halves(backward), high_map, NN)
    own[0] = jnp.where(is_upper, inner_forward, forward)
    own[1] = jnp.where(is_upper, backward, inner_backward)
    sent[0] = jnp.where(is_upper, forward, inner_forward)
    sent[1] = jnp.where(is_upper, inner_backward, backward)


def states_of(blocks, factors, own, arrived, update, source, mats):
    upper = lax.rem(lax.axis_index("seq"), 2) == 1

    def whole(i):
        first = jnp.where(upper, arrived[i], own[i])
        second = jnp.where(upper, own[i], arrived[i])
        return jnp.concatenate([first, second], axis=0)

    before, carried = whole(0), whole(1)
    befores, entries, leaves, totals = [], [], [None] * blocks, [None] * blocks
    for c in range(blocks):
        befores.append(halves(before))
        high, low = befores[-1]
        entry = factors[c] * (dot(high, mats[c], NT) + dot(low, mats[c], NT))
        entries.append(entry)
        before = entry + update[c]
    for c in reversed(range(blocks)):
        leaves[c] = carried
        totals[c] = source[c] + carried
        if c > 0:
            carried = factors[c] * dot_exact(totals[c], mats[c], NN)
    return befores, entries, leaves, totals


def half_terms(blocks, side, factors, entering, update, source, mats):
    half = entering.shape[1]
    rows = pl.ds(pl.multiple_of(side * half, half), half)
    before, carried = entering[0], entering[1]
    befores, totals = [], [None] * blocks
    for c in range(blocks):
        befores.append(halves(before))
        if c + 1 < blocks:
            high, low = befores[c]
            entry = dot(high, mats[c], NT) + dot(low, mats[c], NT)
            before = factors[c, rows, :] * entry + update[c, rows, :]
    for c in reversed(range(blocks)):
        totals[c] = source[c, rows, :] + carried
        if c > 0:
            carried = factors[c, rows, :] * dot_exact(totals[c], mats[c], NN)
    return [
        dot_pair(halves(factors[c, rows, :] * totals[c]), befores[c], TN) for c in range(blocks)
    ]


def own_terms_kernel(blocks, factors, own, update, source, mats, out):
    side = lax.rem(lax.axis_index("seq"), 2)
    for c, term in enumerate(half_terms(blocks, side, factors, own, update, source, mats)):
        out[c] = term


def terms_kernel(
    blocks, ways, factors, own_terms, arrived, update, source, mats, held, sent
):
    head = lax.axis_index("head")
    side = 1 - lax.rem(lax.axis_index("seq"), 2)
    part = STATE // ways
    core = lax.rem(head, 2)
    terms = half_terms(blocks, side, factors, arrived, update, source, mats)
    for c in range(blocks):
        term = own_terms[c] + terms[c]
        for i in range(ways // 2):
            even = term[2 * i * part : (2 * i + 1) * part]
            odd = term[(2 * i + 1) * part : (2 * i + 2) * part]
            held[i, c] = jnp.where(core == 0, even, odd)
            sent[i, c] = jnp.where(core == 0, odd, even)


def rounded_kernel(blocks, factors, own, arrived, update, source, mats, entries, leaves):
    _, entry, leave, _ = states_of(blocks, factors, own, arrived, update, source, mats)
    for c in range(blocks):
        entries[c] = entry[c].astype(BF16)
        leaves[c] = leave[c].astype(BF16)


def regime_kernel(owner, weights, *rest):
    pieces, out = rest[:-1], rest[-1]
    blocks = pieces[0].shape[0]
    for r in range(out.shape[0]):
        total = None
        for i, piece in enumerate(pieces):
            for c in range(blocks):
                at = i * blocks + c
                value = weights[owner, r, at : at + 1, :] * piece[c]
                total = value if total is None else total + value
        out[r] = total


def add_kernel(a, b, out):
    out[...] = a[...] + b[...]


def within_kernel(q, k, v, dy, entries, leaves, *rest):
    dq, dk, dv = rest[-3:]
    row = lax.broadcasted_iota(jnp.int32, (BLOCK, BLOCK), 0)
    column = lax.broadcasted_iota(jnp.int32, (BLOCK, BLOCK), 1)
    lower, upper = row >= column, row <= column
    for h in range(v.shape[1] // HEAD_DIM):
        wide = slice(h * STATE, (h + 1) * STATE)
        narrow = slice(h * HEAD_DIM, (h + 1) * HEAD_DIM)
        qh, kh, vh, gh = q[:, wide], k[:, wide], v[:, narrow], dy[:, narrow]
        entry, leave = entries[0, narrow, :], leaves[0, narrow, :]
        probs_t = jnp.where(upper, dot(kh, qh, NT), 0.0).astype(BF16)
        dscore = jnp.where(lower, dot(gh, vh, NT), 0.0).astype(BF16)
        dscore_t = jnp.where(upper, dot(vh, gh, NT), 0.0).astype(BF16)
        dq[:, wide] = (dot(gh, entry, NN) + dot(dscore, kh, NN)).astype(BF16)
        dk[:, wide] = (dot(vh, leave, NN) + dot(dscore_t, qh, NN)).astype(BF16)
        dv[:, narrow] = (dot(kh, leave, NT) + dot(probs_t, gh, NN)).astype(BF16)


def swap(x, axis, by):
    count = lax.axis_size(axis)
    return lax.ppermute(x, axis, [(i, i ^ by) for i in range(count)])


def level_route(x, distance, parity):
    levels = lax.axis_size("seq") // 2
    pairs = []
    for low in range(levels - distance):
        if (low // distance) % 2 == parity:
            for side in range(2):
                a, b = 2 * low + side, 2 * (low + distance) + side
                pairs += [(a, b), (b, a)]
    return lax.ppermute(x, "seq", pairs)


def routes_up_to(reach, levels):
    return [
        (distance, parity)
        for distance in range(1, reach + 1)
        for parity in range(2)
        if any((low // distance) % 2 == parity for low in range(levels - distance))
    ]


def local(queries, keys, values, out_grad, transitions, gammas, regimes, documents):
    tokens_dev = queries.shape[0]
    heads = gammas.shape[0]
    blocks = tokens_dev // BLOCK
    all_blocks = documents.shape[0]
    devices, ways = lax.axis_size("seq"), lax.axis_size("head")
    levels = devices // 2
    rows = heads * HEAD_DIM
    half = rows // 2
    reach = min(levels - 1, -(-(all_blocks // 2 - 1) // (2 * blocks)))
    routes = routes_up_to(reach, levels)[::-1]
    head = lax.axis_index("head")
    owned, part = REGIMES // devices, STATE // ways
    steps = [devices - 2] + [1 << i for i in range(2, levels.bit_length() - 1)][::-1]
    masks = [0]
    for by in steps:
        masks += [x ^ by for x in masks]

    def shape(*dims, dtype=F32):
        return jax.ShapeDtypeStruct(dims, dtype)

    state_shape = shape(blocks, rows, STATE)
    half_shape = shape(2, half, STATE)
    outs = (state_shape, state_shape, half_shape, half_shape)
    def in_hbm(x):
        return pltpu.with_memory_space_constraint(x, pltpu.HBM)

    def in_vmem(x):
        return pltpu.VMEM(x.shape, x.dtype)

    mat_shape = shape(blocks, STATE, STATE, dtype=BF16)
    inputs = (queries, keys, values, out_grad)
    update, source, sent, held, mats = pl.pallas_call(
        functools.partial(local_kernel, blocks, heads),
        in_specs=[HBM] * 8,
        out_specs=(VMEM,) * 5,
        out_shape=tuple(in_vmem(x) for x in outs + (mat_shape,)),
        scratch_shapes=[in_vmem(x) for x in inputs]
        + [
            pltpu.SMEM(regimes.shape, jnp.int32),
            pltpu.SMEM(documents.shape, jnp.int32),
            pltpu.SMEM(gammas.shape, F32),
            pltpu.SemaphoreType.DMA((3,)),
            pltpu.SemaphoreType.DMA((blocks,)),
            pltpu.SemaphoreType.DMA((2,)),
            pltpu.SemaphoreType.DMA((2, blocks)),
        ],
        compiler_params=PARAMS,
    )(
        *[in_hbm(x) for x in (regimes, documents, gammas, transitions) + inputs]
    )

    arrived = swap(sent, "seq", 1)
    map_shapes = (
        shape(2, 2, STATE, STATE, dtype=BF16),
        shape(reach, rows, 1),
        shape(blocks, rows, 1),
        shape(2, owned, 2 * len(masks) * blocks, STATE),
    )
    if reach > 1:
        map_shapes += (shape(reach - 1, 2, 2, STATE, STATE, dtype=BF16),)
    needed = (2 * reach - 1) * 2 * blocks
    device_maps, powers, factors, weights, *far = pl.pallas_call(
        functools.partial(maps_kernel, blocks, heads, reach, masks),
        in_specs=[SMEM, SMEM, SMEM, HBM],
        out_specs=(VMEM,) * len(map_shapes),
        out_shape=map_shapes,
        scratch_shapes=[
            pltpu.VMEM((needed, STATE, STATE), BF16),
            pltpu.SemaphoreType.DMA((needed,)),
        ],
        compiler_params=PARAMS,
    )(regimes, documents, gammas, in_hbm(transitions))

    trades = pl.pallas_call(
        functools.partial(pair_kernel, routes),
        in_specs=[VMEM] * 4,
        out_specs=(VMEM,) * len(routes),
        out_shape=(shape(half, STATE),) * len(routes),
        compiler_params=PARAMS,
    )(powers, held, arrived, device_maps)
    received = [level_route(x, *route) for x, route in zip(trades, routes)]

    own, sent_entry = pl.pallas_call(
        functools.partial(entry_kernel, reach, routes),
        in_specs=[VMEM] * (4 + len(received) + len(far)),
        out_specs=(VMEM, VMEM),
        out_shape=(half_shape, half_shape),
        compiler_params=PARAMS,
    )(powers, held, arrived, device_maps, *received, *far)
    arrived_entry = swap(sent_entry, "seq", 1)

    part_shape = shape(ways // 2, blocks, part, STATE)
    bf16_states = shape(blocks, rows, STATE, dtype=BF16)
    states = (factors, own, arrived_entry, update, source, mats)

    def states_call(kernel, states, outs, scratch):
        return pl.pallas_call(
            kernel,
            in_specs=[VMEM] * len(states),
            out_specs=(VMEM,) * len(outs),
            out_shape=outs,
            scratch_shapes=scratch,
            compiler_params=PARAMS,
        )(*states)

    (own_terms,) = states_call(
        functools.partial(own_terms_kernel, blocks),
        (factors, own, update, source, mats),
        (shape(blocks, STATE, STATE),),
        [],
    )
    held_term, sent_term = states_call(
        functools.partial(terms_kernel, blocks, ways),
        (factors, own_terms, arrived_entry, update, source, mats),
        (part_shape, part_shape),
        [],
    )

    def output_call(c, entries, leaves, before):
        wide = pl.BlockSpec((BLOCK, 2 * STATE), lambda h: (c, h))
        narrow = pl.BlockSpec((BLOCK, 2 * HEAD_DIM), lambda h: (c, h))
        state = pl.BlockSpec((1, 2 * HEAD_DIM, STATE), lambda h: (c, h, 0))
        return pl.pallas_call(
            within_kernel,
            grid=(heads // 2,),
            in_specs=[wide, wide, narrow, narrow, state, state] + [HBM] * len(before),
            out_specs=[wide, wide, narrow],
            out_shape=[shape(*x.shape, dtype=BF16) for x in inputs[:3]],
            input_output_aliases={6 + i: i for i in range(len(before))},
            compiler_params=PARAMS,
            cost_estimate=pl.CostEstimate(
                flops=20 * heads * BLOCK * BLOCK * STATE,
                bytes_accessed=3 << 20,
                transcendentals=0,
            ),
        )(*[in_hbm(x) for x in inputs], entries, leaves, *before)

    sent_term, states = lax.optimization_barrier((sent_term, states))
    arrived_term = swap(sent_term, "head", 1)
    entries, leaves = states_call(
        functools.partial(rounded_kernel, blocks), states, (bf16_states, bf16_states), []
    )
    arrived_term, entries, leaves = lax.optimization_barrier((arrived_term, entries, leaves))
    summed = held_term + arrived_term
    by, grads = 2, ()
    while by < ways:
        split = summed.reshape(-1, 2, blocks, part, STATE)
        bit = lax.rem(lax.div(head, by), 2)
        going = lax.dynamic_index_in_dim(split, 1 - bit, 1, keepdims=False)
        staying = lax.dynamic_index_in_dim(split, bit, 1, keepdims=False)
        going, entries, leaves = lax.optimization_barrier((going, entries, leaves))
        arrived_part = swap(going, "head", by)
        if not grads:
            grads = output_call(0, entries, leaves, ())
            arrived_part, grads = lax.optimization_barrier((arrived_part, grads))
        summed = staying + arrived_part
        by *= 2
    summed = summed.reshape(blocks, part, STATE)

    pieces = [summed]
    for by in steps:
        pieces += [swap(x, "seq", by) for x in pieces]
    near = swap_near(summed, True)
    pieces += [near] + [swap_near(x, True) for x in pieces[1:]]

    def regime_sum(owner):
        return pl.pallas_call(
            functools.partial(regime_kernel, owner),
            in_specs=[VMEM] * (1 + len(pieces)),
            out_specs=VMEM,
            out_shape=shape(owned, part, STATE),
            compiler_params=PARAMS,
        )(weights, *pieces)

    sent_sum = regime_sum(0)
    sent_sum, grads = lax.optimization_barrier((sent_sum, grads))
    arrived_sum = swap_near(sent_sum, False)
    for c in range(1, blocks):
        grads = output_call(c, entries, leaves, grads)
    own_sum = regime_sum(1)
    arrived_sum, own_sum, grads = lax.optimization_barrier((arrived_sum, own_sum, grads))
    regime_grad = pl.pallas_call(
        add_kernel,
        in_specs=[VMEM, VMEM],
        out_specs=VMEM,
        out_shape=shape(owned, part, STATE),
        compiler_params=PARAMS,
    )(own_sum, arrived_sum)
    return (*grads, regime_grad)


def solution(mesh):
    in_specs = (
        P("seq", "head"),
        P("seq", "head"),
        P("seq", "head"),
        P("seq", "head"),
        P(),
        P("head"),
        P(),
        P(),
    )
    out_specs = (P("seq", "head"), P("seq", "head"), P("seq", "head"), P("seq", "head", None))
    return jax.shard_map(local, mesh=mesh, in_specs=in_specs, out_specs=out_specs, check_vma=False)
```
